256 devices in a mesh: lat: 4 (over y_lo, core), lon: 64 (over z, y_hi, x).
Axes of the slice: x: 4, y: 4 (y_hi: 2, y_lo: 2; y = y_hi * 2 + y_lo), z: 8, core: 2. Of those that a mesh axis runs over, the one named last changes fastest.
Arguments:
- inputs: bfloat16 [2, 192, 768, 512], P(None, 'lat', 'lon'), may hold values from -16 to 16
- cotangent: bfloat16 [2, 192, 768, 512], P(None, 'lat', 'lon'), may hold values from -16 to 16
- w_qkv: bfloat16 [512, 1536], replicated, may hold values from -0.25 to 0.25
- w_out: bfloat16 [512, 512], replicated, may hold values from -0.25 to 0.25
- gain: float32 [512], replicated, may hold values from 0.5 to 1.5
- logit_scale: float32 [16], replicated, may hold values from 2 to 12
Outputs:
- out: bfloat16 [2, 192, 768, 512], P(None, 'lat', 'lon')
- grad_in: bfloat16 [2, 192, 768, 512], P(None, 'lat', 'lon')
- grad_qkv: float32 [512, 1536], P('lon')
- grad_out: float32 [512, 512], P(None, 'lon')
The draws below stay inside these ranges and needn't reach their ends.
All inputs are finite; a program needn't handle non-finite values.
Results may differ from the reference program's by a relative error of at most 0.017.
Values may be sent and summed in bfloat16 or wider, within the bound.
A program may use at most 128 MiB of HBM per device.

```python
import math
import jax
import jax.numpy as jnp
from jax import lax

C = 512
HEADS = 16
WIN_LAT = 6
WIN_LON = 12
SHIFT_LAT = 3
SHIFT_LON = 6
LEV = 2
LAT = 192
LON = 768


def strengthened(drawn, stream_key, source, target, blocks, factor):
    owner, partner = [(jnp.arange(drawn.shape[dim]) // (drawn.shape[dim] // blocks)).reshape([-1 if axis == dim else 1 for axis in range(drawn.ndim)]) for dim in (source, target)]
    chosen = jax.random.permutation(stream_key, blocks)[partner]
    strong = (owner == chosen) | (owner == (partner + blocks // 2) % blocks)
    return jnp.where(strong, factor * drawn, drawn)


def steps_of(stream_key, dims, cuts, least, top_value):
    def one(dim, parts):
        heights = jax.random.uniform(jax.random.fold_in(jax.random.fold_in(stream_key, 6), dim), (parts,), jnp.float32, least / len(cuts), top_value / len(cuts))
        return jnp.repeat(jnp.exp(heights), dims[dim] // parts).reshape((-1,) + (1,) * (len(dims) - dim - 1))

    level = one(*cuts[0])
    for cut in cuts[1:]:
        level = level * one(*cut)
    return level


def normal_values(stream_key, shape, scale, reach, pieces=(), kind=jnp.bfloat16):
    entries = jax.random.normal(stream_key, shape, jnp.float32) * scale
    if len(pieces) > 0:
        entries = steps_of(stream_key, shape, pieces, -0.22, 0.18) * entries
    return jnp.clip(entries, min=-reach, max=reach).astype(kind)


def bell_draw_with(key, shape, scale, most, pieces, heavy, kind=jnp.bfloat16):
    result = scale * jax.random.normal(key, shape, jnp.float32)
    if pieces:
        result = result * steps_of(key, shape, pieces, -0.22, 0.18)
    return jnp.clip(strengthened(result, jax.random.fold_in(key, 3), *heavy), -most, most).astype(kind)


def setup_inputs(seed: int = 0) -> dict:
    splits = jax.random.split(jax.random.key(seed), 7)
    return {
        "inputs": bell_draw_with(splits[0], (LEV, LAT, LON, C), 1.0, 16.0, ((1, 4), (2, 64)), (2, 3, 64, 4.0)),
        "cotangent": bell_draw_with(splits[1], (LEV, LAT, LON, C), 1.0, 16.0, ((1, 4), (2, 64)), (2, 3, 64, 4.0)),
        "w_qkv": normal_values(splits[2], (C, 3 * C), C ** -0.5, 0.25),
        "w_out": normal_values(splits[3], (C, C), C ** -0.5, 0.25),
        "gain": jnp.clip(1.0 + 0.1 * jax.random.normal(splits[4], (C,), jnp.float32), 0.5, 1.5),
        "logit_scale": jnp.clip(jnp.exp(jax.random.uniform(splits[5], (HEADS,), jnp.float32, math.log(2.0), math.log(12.0))), 2.0, 12.0),
    }


norm_floor = 1e-06
norm_eps = 1e-05

def to_windows(grid):
    levels, height, breadth, depth = grid.shape
    blocks = grid.reshape(levels, height // WIN_LAT, WIN_LAT, breadth // WIN_LON, WIN_LON, depth)
    blocks = blocks.transpose(1, 3, 0, 2, 4, 5)
    return blocks.reshape(-1, levels * WIN_LAT * WIN_LON, depth)

def from_windows(windows, levels, height, breadth):
    depth = windows.shape[-1]
    blocks = windows.reshape(height // WIN_LAT, breadth // WIN_LON, levels, WIN_LAT, WIN_LON, depth)
    return blocks.transpose(2, 0, 3, 1, 4, 5).reshape(levels, height, breadth, depth)

def window_pass(x_win, g_win, flag_win, keep_win, w_qkv, w_out, gain, logit_scale):
    tokens, width = x_win.shape
    head_size = width // HEADS
    qkv = jnp.dot(x_win, w_qkv, preferred_element_type=jnp.float32).astype(jnp.bfloat16)
    split = qkv.reshape(tokens, 3, HEADS, head_size)
    query = split[:, 0].astype(jnp.float32)
    key_part = split[:, 1].astype(jnp.float32)
    value_b = split[:, 2]
    q_length = jnp.sqrt(lax.optimization_barrier(jnp.sum(query * query, -1, keepdims=True)))
    k_length = jnp.sqrt(lax.optimization_barrier(jnp.sum(key_part * key_part, -1, keepdims=True)))
    q_radius = jnp.maximum(q_length, norm_floor)
    k_radius = jnp.maximum(k_length, norm_floor)
    unit_q = (query / q_radius).astype(jnp.bfloat16)
    unit_k = (key_part / k_radius).astype(jnp.bfloat16)
    scores = jnp.einsum('ihd,jhd->hij', unit_q.astype(jnp.float32), unit_k.astype(jnp.float32)) * logit_scale[:, None, None]
    allowed = flag_win[:, None] == flag_win[None, :]
    expo = jnp.where(allowed[None], jnp.exp(scores), jnp.zeros_like(scores))
    probs = expo / lax.optimization_barrier(jnp.sum(expo, -1, keepdims=True))
    probs_b = probs.astype(jnp.bfloat16)
    attended = jnp.einsum('hij,jhd->ihd', probs_b.astype(jnp.float32), value_b.astype(jnp.float32))
    attended = attended.reshape(tokens, width).astype(jnp.bfloat16)
    projected = jnp.dot(attended, w_out, preferred_element_type=jnp.float32)
    centre = lax.optimization_barrier(jnp.mean(projected, -1, keepdims=True))
    spread_sq = lax.optimization_barrier(jnp.mean((projected - centre) ** 2, -1, keepdims=True))
    inverse = lax.rsqrt(spread_sq + norm_eps)
    normed = (projected - centre) * inverse
    branch = (gain * normed).astype(jnp.bfloat16)
    upstream = gain * g_win.astype(jnp.float32)
    dproj = (upstream - lax.optimization_barrier(jnp.mean(upstream, -1, keepdims=True)) - normed * lax.optimization_barrier(jnp.mean(upstream * normed, -1, keepdims=True))) * inverse
    dproj_b = dproj.astype(jnp.bfloat16)
    keep_b = keep_win.astype(jnp.bfloat16)[:, None]
    grad_out = jnp.dot((attended * keep_b).T, dproj_b, preferred_element_type=jnp.float32)
    dattended = jnp.dot(dproj_b, w_out.T, preferred_element_type=jnp.float32).astype(jnp.bfloat16)
    dattended = dattended.reshape(tokens, HEADS, head_size)
    dprobs = jnp.einsum('ihd,jhd->hij', dattended.astype(jnp.float32), value_b.astype(jnp.float32))
    dvalue = jnp.einsum('hij,ihd->jhd', probs_b.astype(jnp.float32), dattended.astype(jnp.float32))
    dscores = (probs * (dprobs - lax.optimization_barrier(jnp.sum(probs * dprobs, -1, keepdims=True)))).astype(jnp.bfloat16)
    dunit_q = jnp.einsum('hij,jhd->ihd', dscores.astype(jnp.float32), unit_k.astype(jnp.float32)) * logit_scale[None, :, None]
    dunit_k = jnp.einsum('hij,ihd->jhd', dscores.astype(jnp.float32), unit_q.astype(jnp.float32)) * logit_scale[None, :, None]
    q_tail = jnp.where(q_length > norm_floor, query * lax.optimization_barrier(jnp.sum(query * dunit_q, -1, keepdims=True)) / q_radius ** 3, jnp.zeros_like(query))
    k_tail = jnp.where(k_length > norm_floor, key_part * lax.optimization_barrier(jnp.sum(key_part * dunit_k, -1, keepdims=True)) / k_radius ** 3, jnp.zeros_like(key_part))
    grad_q = dunit_q / q_radius - q_tail
    grad_k = dunit_k / k_radius - k_tail
    dqkv = jnp.stack([grad_q, grad_k, dvalue], axis=1).reshape(tokens, 3 * width).astype(jnp.bfloat16)
    dshifted = jnp.dot(dqkv, w_qkv.T, preferred_element_type=jnp.float32).astype(jnp.bfloat16)
    grad_qkv = jnp.dot((x_win * keep_b).T, dqkv, preferred_element_type=jnp.float32)
    return (branch, dshifted, grad_qkv, grad_out)

def run_windows(x_grid, g_grid, flag_grid, keep_grid, w_qkv, w_out, gain, logit_scale):
    levels, height, breadth, width = x_grid.shape

    def visit(totals, window_item):
        branch, dshifted, grad_qkv, grad_out = window_pass(window_item[0], window_item[1], window_item[2], window_item[3], w_qkv, w_out, gain, logit_scale)
        return ((totals[0] + grad_qkv, totals[1] + grad_out), (branch, dshifted))
    start = (jnp.zeros(w_qkv.shape, jnp.float32), jnp.zeros(w_out.shape, jnp.float32))
    windows = (to_windows(x_grid), to_windows(g_grid), to_windows(flag_grid)[:, :, 0], to_windows(keep_grid)[:, :, 0])
    totals, stacked = lax.scan(visit, start, windows)
    branch = from_windows(stacked[0], levels, height, breadth)
    dshifted = from_windows(stacked[1], levels, height, breadth)
    return (branch, dshifted, totals[0], totals[1])

def reference(inputs, cotangent, w_qkv, w_out, gain, logit_scale):
    shifted = jnp.roll(inputs, (-SHIFT_LAT, -SHIFT_LON), axis=(1, 2))
    shifted_cot = jnp.roll(cotangent, (-SHIFT_LAT, -SHIFT_LON), axis=(1, 2))
    lat_ids = jnp.arange(LAT, dtype=jnp.int32)
    flags = ((lat_ids + SHIFT_LAT) % LAT < SHIFT_LAT).astype(jnp.int32)
    flag_grid = jnp.broadcast_to(flags[None, :, None, None], (LEV, LAT, LON, 1))
    keep_grid = jnp.ones((LEV, LAT, LON, 1), jnp.float32)
    branch, dshifted, grad_qkv, grad_out = run_windows(shifted, shifted_cot, flag_grid, keep_grid, w_qkv, w_out, gain, logit_scale)
    branch_back = jnp.roll(branch, (SHIFT_LAT, SHIFT_LON), axis=(1, 2))
    dshift_back = jnp.roll(dshifted, (SHIFT_LAT, SHIFT_LON), axis=(1, 2))
    out = (inputs.astype(jnp.float32) + branch_back.astype(jnp.float32)).astype(jnp.bfloat16)
    grad_in = (cotangent.astype(jnp.float32) + dshift_back.astype(jnp.float32)).astype(jnp.bfloat16)
    return (out, grad_in, grad_qkv, grad_out)
```

```python
import functools

import jax
import jax.numpy as jnp
from jax import lax
from jax.experimental import pallas as pl
from jax.experimental.pallas import tpu as pltpu
from jax.sharding import PartitionSpec as P

BF = jnp.bfloat16
F32 = jnp.float32
MESH = pl.DeviceIdType.MESH
HEADS = 16
WIDTH = 512
HALF = 72
TOK = 144
QUART = 36
KEYS = 8 * TOK
LOG2E = 1.4426950408889634
FLOOR = 1e-6
EPS = 1e-5


def nn(a, b):
    return jnp.dot(a, b, preferred_element_type=F32)


def nt(a, b):
    return lax.dot_general(a, b, (((1,), (1,)), ((), ())), preferred_element_type=F32)


def tn(a, b):
    return lax.dot_general(a, b, (((0,), (0,)), ((), ())), preferred_element_type=F32)


def spread(part):
    head = lax.broadcasted_iota(jnp.int32, part.shape, 1) // 32
    zero = jnp.zeros_like(part)
    return jnp.concatenate([jnp.where(head == h, part, zero) for h in range(8)], axis=0)


def head_sum(value, ones_block):
    return nn(value.astype(BF), ones_block)


def head_sum_fine(value, ones_block):
    high = value.astype(BF)
    low = (value - high.astype(F32)).astype(BF)
    return nn(high, ones_block) + nn(low, ones_block)


def window_math(xw, gw, split, w_qkv, w_out, gain, scale_cols, scale_lanes, ones_big, ones_blk, qkv):
    qkv[...] = nn(xw, w_qkv[...]).astype(BF)
    ones_block = ones_blk[...]
    row = lax.broadcasted_iota(jnp.int32, (TOK, 1), 0)
    col = lax.broadcasted_iota(jnp.int32, (1, KEYS), 1)
    row_flag = jnp.where(split, (row // QUART) % 2, 0)
    col_flag = jnp.where(split, (col // QUART) % 2, 0)
    allowed = row_flag == col_flag
    att = []
    saved = []
    for half in range(2):
        lo = half * 256
        q = qkv[:, lo : lo + 256].astype(F32)
        k = qkv[:, 512 + lo : 768 + lo].astype(F32)
        v = qkv[:, 1024 + lo : 1280 + lo]
        q_len = jnp.sqrt(head_sum_fine(q * q, ones_block))
        k_len = jnp.sqrt(head_sum_fine(k * k, ones_block))
        q_inv = 1.0 / jnp.maximum(q_len, FLOOR)
        k_inv = 1.0 / jnp.maximum(k_len, FLOOR)
        uq = (q * q_inv).astype(BF)
        uk = (k * k_inv).astype(BF)
        scl = scale_cols[half : half + 1, :]
        k_big = spread(uk)
        e = jnp.exp2(nt(uq, k_big) * scl)
        e = jnp.where(allowed, e, 0.0).astype(BF)
        v_big = spread(v)
        r_den = 1.0 / nn(e, ones_big[...])
        att.append((nn(e, v_big) * r_den).astype(BF))
        saved.append((q, k, v, q_len, k_len, q_inv, k_inv, uq, uk, k_big, v_big, e, r_den, scl))
    att_b = jnp.concatenate(att, axis=1)
    proj = nn(att_b, w_out[...])
    dev = proj - jnp.mean(proj, -1, keepdims=True)
    inv = lax.rsqrt(jnp.mean(dev * dev, -1, keepdims=True) + EPS)
    normed = dev * inv
    branch = gain * normed
    up = gain * gw
    dproj = (
        (up - jnp.mean(up, -1, keepdims=True) - normed * jnp.mean(up * normed, -1, keepdims=True))
        * inv
    ).astype(BF)
    datt = nt(dproj, w_out[...]).astype(BF)
    dq, dk, dv = [], [], []
    for half in range(2):
        lo = half * 256
        q, k, v, q_len, k_len, q_inv, k_inv, uq, uk, k_big, v_big, e, r_den, scl = saved[half]
        dh = datt[:, lo : lo + 256].astype(F32) * r_den
        dh_b = dh.astype(BF)
        dd = (dh * att[half].astype(F32)).astype(BF)
        t = nt(dh_b, v_big) - nt(dd, ones_big[...])
        ds = (e.astype(F32) * t).astype(BF)
        lanes = scale_lanes[half : half + 1, :]
        duq = nn(ds, k_big) * lanes
        q_big = spread(uq)
        et = jnp.exp2(nt(uk, q_big) * scl)
        et = jnp.where(allowed, et, 0.0).astype(BF)
        d_big = spread(dh_b)
        dd_big = spread(dd)
        tt = nt(v, d_big) - nt(jnp.ones((TOK, 256), BF), dd_big)
        dst = (et.astype(F32) * tt).astype(BF)
        duk = nn(dst, q_big) * lanes
        qn = q * q_inv
        kn = k * k_inv
        q_tail = jnp.where(q_len > FLOOR, qn * head_sum(qn * duq, ones_block), 0.0)
        k_tail = jnp.where(k_len > FLOOR, kn * head_sum(kn * duk, ones_block), 0.0)
        dq.append(((duq - q_tail) * q_inv).astype(BF))
        dk.append(((duk - k_tail) * k_inv).astype(BF))
        dv.append(nn(et, d_big).astype(BF))
    dqkv = jnp.concatenate(dq + dk + dv, axis=1)
    dshifted = nt(dqkv, w_qkv[...])
    return branch, dshifted, att_b, dproj, dqkv


def pack(ref, rows, first_col):
    parts = []
    for r in rows:
        for lev in range(2):
            parts.append(ref[lev, r].astype(F32)[first_col : first_col + 6])
    return jnp.concatenate(parts, axis=0)


def piece_of(x_part, g_part):
    pad = jnp.zeros((4, WIDTH), F32)
    return jnp.concatenate([x_part, pad, g_part, pad], axis=0).astype(BF)


def unpiece(ref):
    whole = ref.astype(F32)
    return whole[:QUART], whole[40 : 40 + QUART]


def attention_kernel(
    x_ref,
    g_ref,
    w_qkv,
    w_out,
    gain_ref,
    scale_cols,
    scale_lanes,
    ones_big,
    ones_blk,
    out_ref,
    gin_ref,
    grads_ref,
    send,
    recv,
    own,
    back_send,
    back_recv,
    own_res,
    send7,
    recv7,
    back7_send,
    back7_recv,
    qkv,
    x_all,
    att_all,
    dproj_all,
    dqkv_all,
    send_sem,
    recv_sem,
    back_send_sem,
    back_recv_sem,
    send7_sem,
    recv7_sem,
    back7_send_sem,
    back7_recv_sem,
):
    n_lat = lax.axis_size("lat")
    n_lon = lax.axis_size("lon")
    a = lax.axis_index("lat")
    b = lax.axis_index("lon")
    up_a = lax.rem(a + 1, n_lat)
    dn_a = lax.rem(a + n_lat - 1, n_lat)
    up_b = lax.rem(b + 1, n_lon)
    dn_b = lax.rem(b + n_lon - 1, n_lon)

    barrier = pltpu.get_barrier_semaphore()
    for peer in ((a, up_b), (a, dn_b), (up_a, b), (dn_a, b), (up_a, dn_b), (dn_a, up_b)):
        pl.semaphore_signal(barrier, inc=1, device_id=peer, device_id_type=MESH)
    pl.semaphore_wait(barrier, 6)

    def forth(w, peer):
        return pltpu.make_async_remote_copy(
            src_ref=send.at[w],
            dst_ref=recv.at[w],
            send_sem=send_sem.at[w],
            recv_sem=recv_sem.at[w],
            device_id=peer,
            device_id_type=MESH,
        )

    def back(w, peer):
        return pltpu.make_async_remote_copy(
            src_ref=back_send.at[w],
            dst_ref=back_recv.at[w],
            send_sem=back_send_sem.at[w],
            recv_sem=back_recv_sem.at[w],
            device_id=peer,
            device_id_type=MESH,
        )

    def forth7(j):
        return pltpu.make_async_remote_copy(
            src_ref=send7.at[j],
            dst_ref=recv7.at[j],
            send_sem=send7_sem.at[j],
            recv_sem=recv7_sem.at[j],
            device_id=((a, up_b), (dn_a, b), (dn_a, up_b))[j],
            device_id_type=MESH,
        )

    def back7(j):
        return pltpu.make_async_remote_copy(
            src_ref=back7_send.at[j],
            dst_ref=back7_recv.at[j],
            send_sem=back7_send_sem.at[j],
            recv_sem=back7_recv_sem.at[j],
            device_id=((a, dn_b), (up_a, b), (up_a, dn_b))[j],
            device_id_type=MESH,
        )

    def both(w, first_col):
        rows = [6 * w + 3 + i for i in range(6)]
        return jnp.concatenate(
            [pack(x_ref, rows, first_col), pack(g_ref, rows, first_col)], axis=0
        ).astype(BF)

    @pl.loop(0, 4)
    def _(pair):
        w = 2 * pair
        send[w] = both(w, 0)
        forth(w, (a, dn_b)).start()

        @pl.when(pair < 3)
        def _():
            send[w + 1] = both(w + 1, 6)
            forth(w + 1, (a, up_b)).start()

    low_rows = [45, 46, 47]
    top_rows = [0, 1, 2]
    for j, (rows, first_col) in enumerate(((low_rows, 6), (top_rows, 0), (top_rows, 6))):
        send7[j] = piece_of(pack(x_ref, rows, first_col), pack(g_ref, rows, first_col))
        forth7(j).start()

    @pl.loop(0, 4)
    def _(pair):
        w = 2 * pair
        own[w] = both(w, 6)

        @pl.when(pair < 3)
        def _():
            own[w + 1] = both(w + 1, 0)

    @pl.loop(0, 8)
    def _(w):
        @pl.when(w < 7)
        def _():
            forth(w, (a, up_b)).wait_recv()

        @pl.when(w == 7)
        def _():
            for j in range(3):
                forth7(j).wait_recv()
            low_x = pack(x_ref, low_rows, 0)
            low_g = pack(g_ref, low_rows, 0)
            side_x, side_g = unpiece(recv7[0])
            down_x, down_g = unpiece(recv7[1])
            diag_x, diag_g = unpiece(recv7[2])
            own[7] = jnp.concatenate([low_x, down_x, low_g, down_g], axis=0).astype(BF)
            recv[7] = jnp.concatenate([side_x, diag_x, side_g, diag_g], axis=0).astype(BF)

        mine = own[w].astype(F32)
        theirs = recv[w].astype(F32)
        xw = jnp.concatenate([mine[:HALF], theirs[:HALF]], axis=0).astype(BF)
        gw = jnp.concatenate([mine[HALF:], theirs[HALF:]], axis=0)
        split = jnp.logical_and(w == 7, a == n_lat - 1)
        branch, dshifted, att, dproj, dqkv = window_math(
            xw, gw, split, w_qkv, w_out, gain_ref[...], scale_cols, scale_lanes, ones_big, ones_blk, qkv
        )
        own_res[w] = jnp.concatenate([branch[:HALF], dshifted[:HALF]], axis=0).astype(BF)
        back_send[w] = jnp.concatenate([branch[HALF:], dshifted[HALF:]], axis=0).astype(BF)

        @pl.when(w < 7)
        def _():
            odd = lax.rem(w, 2)
            back(w, (a, up_b * (1 - odd) + dn_b * odd)).start()

        rows = pl.ds(pl.multiple_of(w * TOK, TOK), TOK)
        x_all[rows, :] = xw
        att_all[rows, :] = att
        dproj_all[rows, :] = dproj
        dqkv_all[rows, :] = dqkv

    mine = own_res[7].astype(F32)
    theirs = back_send[7].astype(F32)
    back7_send[0] = piece_of(theirs[:QUART], theirs[HALF : HALF + QUART])
    back7_send[1] = piece_of(mine[QUART:HALF], mine[HALF + QUART :])
    back7_send[2] = piece_of(theirs[QUART:HALF], theirs[HALF + QUART :])
    for j in range(3):
        back7(j).start()

    def column(c):
        if c < 6:
            return tn(x_all[...], dqkv_all[:, c * 256 : (c + 1) * 256])
        return tn(dproj_all[...], att_all[:, (c - 6) * 256 : (c - 5) * 256])

    for part in range(4):
        core, y_lo = part // 2, part % 2
        first = column(part).reshape(64, 8, 256)
        second = column(part + 4).reshape(64, 8, 256)
        joined = jnp.concatenate([first, second], axis=1).astype(BF)
        for lon in range(64):
            z, y, x = lon // 8, 2 * ((lon // 4) % 2) + y_lo, lon % 4
            u, v = (x, y) if core == 0 else (y, x)
            grads_ref[core, u, v, z] = joined[lon]

    def assemble(rows, left_b, right_b, left_d, right_d):
        for i, r in enumerate(rows):
            for lev in range(2):
                at = (2 * i + lev) * 6
                branch = jnp.concatenate([left_b[at : at + 6], right_b[at : at + 6]], axis=0)
                dshift = jnp.concatenate([left_d[at : at + 6], right_d[at : at + 6]], axis=0)
                out_ref[lev, r] = (x_ref[lev, r].astype(F32) + branch).astype(BF)
                gin_ref[lev, r] = (g_ref[lev, r].astype(F32) + dshift).astype(BF)

    @pl.loop(0, 4)
    def _(pair):
        w = 2 * pair
        back(w, (a, up_b)).wait_recv()
        mine = own_res[w].astype(F32)
        came = back_recv[w].astype(F32)
        assemble([6 * w + 3 + i for i in range(6)], came[:HALF], mine[:HALF], came[HALF:], mine[HALF:])

        @pl.when(pair < 3)
        def _():
            v = w + 1
            back(v, (a, up_b)).wait_recv()
            mine = own_res[v].astype(F32)
            came = back_recv[v].astype(F32)
            assemble(
                [6 * v + 3 + i for i in range(6)], mine[:HALF], came[:HALF], mine[HALF:], came[HALF:]
            )

    for j in range(3):
        back7(j).wait_recv()
    mine = own_res[7].astype(F32)
    side_b, side_d = unpiece(back7_recv[0])
    down_b, down_d = unpiece(back7_recv[1])
    diag_b, diag_d = unpiece(back7_recv[2])
    assemble(low_rows, mine[:QUART], side_b, mine[HALF : HALF + QUART], side_d)
    assemble(top_rows, down_b, diag_b, down_d, diag_d)

    @pl.loop(0, 7)
    def _(w):
        forth(w, (a, up_b)).wait_send()
        back(w, (a, up_b)).wait_send()

    for j in range(3):
        forth7(j).wait_send()
        back7(j).wait_send()


def reduce_kernel(
    grads_ref,
    gq_ref,
    go_ref,
    pair_recv,
    mine,
    ring_relay,
    ring_recv,
    cut,
    line_recv,
    piece,
    z_recv,
    part,
    whole,
    pair_send_sem,
    pair_recv_sem,
    relay_send_sem,
    relay_recv_sem,
    ring_send_sem,
    ring_recv_sem,
    line_send_sem,
    line_recv_sem,
    z_send_sem,
    z_recv_sem,
    gather_send_sem,
    gather_recv_sem,
):
    lat = lax.axis_index("lat")
    lon = lax.axis_index("lon")
    core, y_lo = lax.rem(lat, 2), lat // 2
    z, y_hi, x = lon // 8, lax.rem(lon // 4, 2), lax.rem(lon, 4)
    y = 2 * y_hi + y_lo
    u = x * (1 - core) + y * core
    v = y * (1 - core) + x * core
    other_u = y * (1 - core) + x * core

    def device(uu, vv, zz):
        xx = uu * (1 - core) + vv * core
        yy = vv * (1 - core) + uu * core
        return (2 * lax.rem(yy, 2) + core, zz * 8 + (yy // 2) * 4 + xx)

    def mod(value, n):
        return lax.rem(value + n, n)

    partner = (lat + 1 - 2 * core, lon)
    nxt = device(mod(u + 1, 4), v, z)
    prv = device(mod(u + 3, 4), v, z)
    line = [device(u, mod(v + i, 4), z) for i in range(1, 4)]
    column = [device(u, v, mod(z + i, 8)) for i in range(1, 8)]
    group = [(mod(lat + i, 4), lon) for i in range(1, 4)]
    peers = [partner, nxt, prv] + line + column + group
    barrier = pltpu.get_barrier_semaphore()
    for peer in peers:
        pl.semaphore_signal(barrier, inc=1, device_id=peer, device_id_type=MESH)
    pl.semaphore_wait(barrier, len(peers))

    def copy(src, dst, send_sem, recv_sem, peer):
        return pltpu.make_async_remote_copy(
            src_ref=src, dst_ref=dst, send_sem=send_sem, recv_sem=recv_sem, device_id=peer, device_id_type=MESH
        )

    order = (2, 1, 3, 0)
    pair = []
    for i, step in enumerate(order):
        chunk = mod(other_u + step, 4)
        c = copy(
            grads_ref.at[1 - core, chunk],
            pair_recv.at[i],
            pair_send_sem.at[i],
            pair_recv_sem.at[i],
            partner,
        )
        c.start()
        pair.append(c)

    def add_pair(i):
        pair[i].wait_recv()
        chunk = mod(u + order[i], 4)

        @pl.loop(0, 4)
        def _(vv):
            mine[i, vv] = (
                grads_ref[core, chunk, vv].astype(F32) + pair_recv[i, vv].astype(F32)
            ).astype(BF)

    add_pair(0)
    relay_up = copy(mine.at[0, pl.ds(0, 2)], ring_relay.at[0], relay_send_sem.at[0], relay_recv_sem.at[0], nxt)
    relay_dn = copy(mine.at[0, pl.ds(2, 2)], ring_relay.at[1], relay_send_sem.at[1], relay_recv_sem.at[1], prv)
    relay_up.start()
    relay_dn.start()
    add_pair(1)
    up_b = copy(mine.at[1, pl.ds(2, 2)], ring_recv.at[0, pl.ds(2, 2)], ring_send_sem.at[0], ring_recv_sem.at[0], nxt)
    up_b.start()
    add_pair(2)
    dn_a = copy(mine.at[2, pl.ds(0, 2)], ring_recv.at[1, pl.ds(0, 2)], ring_send_sem.at[1], ring_recv_sem.at[1], prv)
    dn_a.start()
    add_pair(3)
    relay_up.wait_recv()

    @pl.loop(0, 2)
    def _(vv):
        mine[1, vv] = (mine[1, vv].astype(F32) + ring_relay[0, vv].astype(F32)).astype(BF)

    up_a = copy(mine.at[1, pl.ds(0, 2)], ring_recv.at[0, pl.ds(0, 2)], ring_send_sem.at[2], ring_recv_sem.at[2], nxt)
    up_a.start()
    relay_dn.wait_recv()

    @pl.loop(0, 2)
    def _(vv):
        mine[2, 2 + vv] = (mine[2, 2 + vv].astype(F32) + ring_relay[1, vv].astype(F32)).astype(BF)

    dn_b = copy(mine.at[2, pl.ds(2, 2)], ring_recv.at[1, pl.ds(2, 2)], ring_send_sem.at[3], ring_recv_sem.at[3], prv)
    dn_b.start()
    for c in (up_b, dn_a, up_a, dn_b):
        c.wait_recv()

    @pl.loop(0, 4)
    def _(vv):
        cut[vv] = (
            mine[3, vv].astype(F32) + ring_recv[0, vv].astype(F32) + ring_recv[1, vv].astype(F32)
        ).astype(BF)

    lines = []
    for i in range(1, 4):
        c = copy(
            cut.at[mod(v + i, 4)], line_recv.at[i - 1], line_send_sem.at[i - 1], line_recv_sem.at[i - 1], line[i - 1]
        )
        c.start()
        lines.append(c)
    for c in lines:
        c.wait_recv()
    piece[...] = (
        cut[v].astype(F32) + line_recv[0].astype(F32) + line_recv[1].astype(F32) + line_recv[2].astype(F32)
    ).astype(BF)
    columns = []
    for i in range(1, 8):
        c = copy(
            piece.at[mod(z + i, 8)], z_recv.at[i - 1], z_send_sem.at[i - 1], z_recv_sem.at[i - 1], column[i - 1]
        )
        c.start()
        columns.append(c)
    for c in columns:
        c.wait_recv()
    total = piece[z].astype(F32)
    for i in range(7):
        total = total + z_recv[i].astype(F32)
    part[...] = total

    here = 2 * core + y_lo
    whole[here] = total
    gathers = []
    for i in range(1, 4):
        c = copy(part, whole.at[here], gather_send_sem.at[i - 1], gather_recv_sem.at[i - 1], group[i - 1])
        c.start()
        gathers.append(c)
    for c in gathers:
        c.wait_recv()
    for p in range(4):
        gq_ref[:, p * 256 : (p + 1) * 256] = whole[p, 0:8, :]
        if p < 2:
            gq_ref[:, 1024 + p * 256 : 1280 + p * 256] = whole[p, 8:16, :]
        else:
            go_ref[:, (p - 2) * 256 : (p - 1) * 256] = whole[p, 8:16, :]
    for c in pair + [relay_up, relay_dn, up_b, dn_a, up_a, dn_b] + lines + columns + gathers:
        c.wait_send()


def body(inputs, cotangent, w_qkv, w_out, gain, logit_scale):
    vmem = pl.BlockSpec(memory_space=pltpu.VMEM)
    scale_cols = jnp.repeat((logit_scale * LOG2E).reshape(2, 8), TOK, axis=1)
    scale_lanes = jnp.repeat(logit_scale.reshape(2, 8), 32, axis=1)
    head = jnp.arange(256) // 32
    ones_blk = (head[:, None] == head[None, :]).astype(BF)
    ones_big = ((jnp.arange(KEYS) // TOK)[:, None] == head[None, :]).astype(BF)
    dma = pltpu.SemaphoreType.DMA
    blocks = pltpu.VMEM((8, TOK, WIDTH), BF)
    pieces = pltpu.VMEM((3, 80, WIDTH), BF)
    out, grad_in, grads = pl.pallas_call(
        attention_kernel,
        out_shape=[
            jax.ShapeDtypeStruct(inputs.shape, BF),
            jax.ShapeDtypeStruct(inputs.shape, BF),
            jax.ShapeDtypeStruct((2, 4, 4, 8, 16, 256), BF),
        ],
        in_specs=[vmem] * 9,
        out_specs=[vmem] * 3,
        scratch_shapes=[blocks] * 6
        + [pieces] * 4
        + [
            pltpu.VMEM((TOK, 3 * WIDTH), BF),
            pltpu.VMEM((8 * TOK, WIDTH), BF),
            pltpu.VMEM((8 * TOK, WIDTH), BF),
            pltpu.VMEM((8 * TOK, WIDTH), BF),
            pltpu.VMEM((8 * TOK, 3 * WIDTH), BF),
        ]
        + [dma((7,))] * 4
        + [dma((3,))] * 4,
        compiler_params=pltpu.CompilerParams(
            collective_id=0, has_side_effects=True, vmem_limit_bytes=56 * 2**20
        ),
    )(inputs, cotangent, w_qkv, w_out, gain.reshape(1, WIDTH), scale_cols, scale_lanes, ones_big, ones_blk)
    share_qkv, share_out = pl.pallas_call(
        reduce_kernel,
        out_shape=[jax.ShapeDtypeStruct((8, 1536), F32), jax.ShapeDtypeStruct((8, 512), F32)],
        in_specs=[vmem],
        out_specs=[vmem] * 2,
        scratch_shapes=[
            pltpu.VMEM((4, 4, 8, 16, 256), BF),
            pltpu.VMEM((4, 4, 8, 16, 256), BF),
            pltpu.VMEM((2, 2, 8, 16, 256), BF),
            pltpu.VMEM((2, 4, 8, 16, 256), BF),
            pltpu.VMEM((4, 8, 16, 256), BF),
            pltpu.VMEM((3, 8, 16, 256), BF),
            pltpu.VMEM((8, 16, 256), BF),
            pltpu.VMEM((7, 16, 256), BF),
            pltpu.VMEM((16, 256), F32),
            pltpu.VMEM((4, 16, 256), F32),
        ]
        + [dma((4,))] * 2
        + [dma((2,))] * 2
        + [dma((4,))] * 2
        + [dma((3,))] * 2
        + [dma((7,))] * 2
        + [dma((3,))] * 2,
        compiler_params=pltpu.CompilerParams(
            collective_id=1, has_side_effects=True, vmem_limit_bytes=32 * 2**20
        ),
    )(grads)
    return out, grad_in, share_qkv, share_out.T


def solution(mesh):
    placed = (P(None, "lat", "lon", None), P(None, "lat", "lon", None), P(), P(), P(), P())
    return jax.shard_map(
        body,
        mesh=mesh,
        in_specs=placed,
        out_specs=(
            P(None, "lat", "lon", None),
            P(None, "lat", "lon", None),
            P("lon", None),
            P(None, "lon"),
        ),
        check_vma=False,
    )
```

```python
import jax
import jax.numpy as jnp
from jax import lax
from jax.experimental import pallas as pl
from jax.experimental.pallas import tpu as pltpu
from jax.sharding import PartitionSpec as P

BF = jnp.bfloat16
F32 = jnp.float32
MESH = pl.DeviceIdType.MESH
HEADS = 16
WIDTH = 512
HALF = 72
TOK = 144
QUART = 36
KEYS = 8 * TOK
LOG2E = 1.4426950408889634
FLOOR = 1e-6
EPS = 1e-5


def nn(a, b):
    return jnp.dot(a, b, preferred_element_type=F32)


def nt(a, b):
    return lax.dot_general(a, b, (((1,), (1,)), ((), ())), preferred_element_type=F32)


def tn(a, b):
    return lax.dot_general(a, b, (((0,), (0,)), ((), ())), preferred_element_type=F32)


def spread(part):
    head = lax.broadcasted_iota(jnp.int32, part.shape, 1) // 32
    zero = jnp.zeros_like(part)
    return jnp.concatenate([jnp.where(head == h, part, zero) for h in range(8)], axis=0)


def pick(full):
    head = lax.broadcasted_iota(jnp.int32, (TOK, 256), 1) // 32
    chosen = full[:TOK]
    for h in range(1, 8):
        chosen = jnp.where(head == h, full[h * TOK : (h + 1) * TOK], chosen)
    return chosen


def head_sum(value, ones_block):
    return nn(value.astype(BF), ones_block)


def head_sum_fine(value, ones_block):
    high = value.astype(BF)
    low = (value - high.astype(F32)).astype(BF)
    return nn(high, ones_block) + nn(low, ones_block)


def pair_math(x, gw, split, w_qkv, w_qkv_t, w_out, w_out_t, gain, scale_cols, scale_lanes, ones_big, ones_big_t, ones_blk):
    ones_block = ones_blk[...]
    qkv = nn(x, w_qkv[...]).astype(BF)
    row = lax.broadcasted_iota(jnp.int32, (TOK, 1), 0)
    col = lax.broadcasted_iota(jnp.int32, (1, KEYS), 1)
    allowed = jnp.where(split, (row // QUART) % 2, 0) == jnp.where(split, (col // QUART) % 2, 0)
    vec = []
    for half in range(2):
        lo = half * 256
        q = qkv[:, lo : lo + 256].astype(F32)
        k = qkv[:, 512 + lo : 768 + lo].astype(F32)
        q_len = jnp.sqrt(head_sum_fine(q * q, ones_block))
        k_len = jnp.sqrt(head_sum_fine(k * k, ones_block))
        q_inv = 1.0 / jnp.maximum(q_len, FLOOR)
        k_inv = 1.0 / jnp.maximum(k_len, FLOOR)
        uq = q * q_inv
        uk = k * k_inv
        vec.append((q_len, k_len, q_inv, k_inv, uq, uk, uq.astype(BF), uk.astype(BF)))
    att = [[None, None], [None, None]]
    saved = {}
    for g in range(2):
        r = slice(g * TOK, (g + 1) * TOK)
        for half in range(2):
            lo = half * 256
            uq, uk = vec[half][6][r], vec[half][7][r]
            k_big = spread(uk)
            v_big = spread(qkv[r, 1024 + lo : 1280 + lo])
            e = jnp.exp2(nt(uq, k_big) * scale_cols[half : half + 1, :])
            if g == 1:
                e = jnp.where(allowed, e, 0.0)
            e = e.astype(BF)
            both = nn(e, jnp.concatenate([v_big, ones_big[...]], axis=1))
            r_den = 1.0 / both[:, 256:]
            att[g][half] = (both[:, :256] * r_den).astype(BF)
            saved[g, half] = (k_big, v_big, e, r_den, uq)
    att_b = jnp.concatenate([jnp.concatenate(one, axis=1) for one in att], axis=0)
    proj = nn(att_b, w_out[...])
    dev = proj - jnp.mean(proj, -1, keepdims=True)
    inv = lax.rsqrt(jnp.mean(dev * dev, -1, keepdims=True) + EPS)
    normed = dev * inv
    branch = gain * normed
    up = gain * gw
    dproj = (
        (up - jnp.mean(up, -1, keepdims=True) - normed * jnp.mean(up * normed, -1, keepdims=True))
        * inv
    ).astype(BF)
    datt = nn(dproj, w_out_t[...]).astype(BF)
    dq, dk, dv = {}, {}, {}
    for g in range(2):
        r = slice(g * TOK, (g + 1) * TOK)
        for half in range(2):
            lo = half * 256
            k_big, v_big, e, r_den, uq = saved[g, half]
            dh = datt[r, lo : lo + 256].astype(F32) * r_den
            dh_b = dh.astype(BF)
            dd = (dh * att[g][half].astype(F32)).astype(BF)
            t = nt(dh_b, v_big) - nn(dd, ones_big_t[...])
            ds = (e.astype(F32) * t).astype(BF)
            lanes = scale_lanes[half : half + 1, :]
            dq[g, half] = nn(ds, k_big) * lanes
            dk[g, half] = pick(tn(ds, uq)) * lanes
            dv[g, half] = pick(tn(e, dh_b)).astype(BF)
    cols = [None] * 6
    for half in range(2):
        q_len, k_len, q_inv, k_inv, uq, uk, _, _ = vec[half]
        duq = jnp.concatenate([dq[0, half], dq[1, half]], axis=0)
        duk = jnp.concatenate([dk[0, half], dk[1, half]], axis=0)
        q_tail = jnp.where(q_len > FLOOR, uq * head_sum(uq * duq, ones_block), 0.0)
        k_tail = jnp.where(k_len > FLOOR, uk * head_sum(uk * duk, ones_block), 0.0)
        cols[half] = ((duq - q_tail) * q_inv).astype(BF)
        cols[2 + half] = ((duk - k_tail) * k_inv).astype(BF)
        cols[4 + half] = jnp.concatenate([dv[0, half], dv[1, half]], axis=0)
    dqkv = jnp.concatenate(cols, axis=1)
    dshifted = nn(dqkv, w_qkv_t[...])
    return branch, dshifted, att_b, dproj, dqkv


def pack(ref, first_row, rows, first_col):
    low = first_row // 16 * 16
    high = (first_row + rows + 15) // 16 * 16
    parts = []
    for lev in range(2):
        for c in range(first_col, first_col + 6):
            strip = ref[lev, c, low:high, :].astype(F32)
            parts.append(strip[first_row - low : first_row - low + rows])
    return jnp.concatenate(parts, axis=0)


def piece_of(x_part, g_part):
    pad = jnp.zeros((4, WIDTH), F32)
    return jnp.concatenate([x_part, pad, g_part, pad], axis=0).astype(BF)


def unpiece(ref):
    whole = ref.astype(F32)
    return whole[:QUART], whole[40 : 40 + QUART]


def block_kernel(
    x_ref,
    g_ref,
    w_qkv,
    w_out,
    gain_ref,
    scale_ref,
    out_ref,
    gin_ref,
    gq_ref,
    go_ref,
    send,
    recv,
    own,
    back_send,
    back_recv,
    own_res,
    send7,
    recv7,
    back7_send,
    back7_recv,
    x_all,
    att_all,
    dproj_all,
    dqkv_all,
    w_qkv_t,
    w_out_t,
    ones_big,
    ones_big_t,
    ones_blk,
    scale_cols,
    scale_lanes,
    grads,
    pair_recv,
    mine,
    ring_relay,
    ring_recv,
    cut,
    line_recv,
    piece,
    z_recv,
    part,
    whole,
    send_sem,
    recv_sem,
    back_send_sem,
    back_recv_sem,
    send7_sem,
    recv7_sem,
    back7_send_sem,
    back7_recv_sem,
    pair_send_sem,
    pair_recv_sem,
    relay_send_sem,
    relay_recv_sem,
    ring_send_sem,
    ring_recv_sem,
    line_send_sem,
    line_recv_sem,
    z_send_sem,
    z_recv_sem,
    gather_send_sem,
    gather_recv_sem,
):
    n_lat = lax.axis_size("lat")
    n_lon = lax.axis_size("lon")
    a = lax.axis_index("lat")
    b = lax.axis_index("lon")

    def mod(value, n):
        return lax.rem(value + n, n)

    up_a, dn_a = mod(a + 1, n_lat), mod(a - 1, n_lat)
    up_b, dn_b = mod(b + 1, n_lon), mod(b - 1, n_lon)
    core, y_lo = lax.rem(a, 2), a // 2
    z, y_hi, x = b // 8, lax.rem(b // 4, 2), lax.rem(b, 4)
    y = 2 * y_hi + y_lo
    u = x * (1 - core) + y * core
    v = y * (1 - core) + x * core

    def device(uu, vv, zz):
        xx = uu * (1 - core) + vv * core
        yy = vv * (1 - core) + uu * core
        return (2 * lax.rem(yy, 2) + core, zz * 8 + (yy // 2) * 4 + xx)

    partner = (a + 1 - 2 * core, b)
    nxt = device(mod(u + 1, 4), v, z)
    prv = device(mod(u + 3, 4), v, z)
    line = [device(u, mod(v + i, 4), z) for i in range(1, 4)]
    column = [device(u, v, mod(z + i, 8)) for i in range(1, 8)]
    group = [(mod(a + i, 4), b) for i in range(1, 4)]
    around = [(a, up_b), (a, dn_b), (up_a, b), (dn_a, b), (up_a, dn_b), (dn_a, up_b)]
    peers = around + [partner, nxt, prv] + line + column + group

    barrier = pltpu.get_barrier_semaphore()
    for peer in peers:
        pl.semaphore_signal(barrier, inc=1, device_id=peer, device_id_type=MESH)

    def copy(src, dst, send_sem, recv_sem, peer):
        return pltpu.make_async_remote_copy(
            src_ref=src, dst_ref=dst, send_sem=send_sem, recv_sem=recv_sem, device_id=peer, device_id_type=MESH
        )

    def forth(w, peer):
        return copy(send.at[w], recv.at[w], send_sem.at[w], recv_sem.at[w], peer)

    def back(w, peer):
        return copy(back_send.at[w], back_recv.at[w], back_send_sem.at[w], back_recv_sem.at[w], peer)

    def forth7(j):
        peer = ((a, up_b), (dn_a, b), (dn_a, up_b))[j]
        return copy(send7.at[j], recv7.at[j], send7_sem.at[j], recv7_sem.at[j], peer)

    def back7(j):
        peer = ((a, dn_b), (up_a, b), (up_a, dn_b))[j]
        return copy(back7_send.at[j], back7_recv.at[j], back7_send_sem.at[j], back7_recv_sem.at[j], peer)

    def both(w, first_col):
        return jnp.concatenate(
            [pack(x_ref, 6 * w + 3, 6, first_col), pack(g_ref, 6 * w + 3, 6, first_col)], axis=0
        ).astype(BF)

    for w in range(7):
        send[w] = both(w, 6 * (w % 2))
        if w == 0:
            pl.semaphore_wait(barrier, len(peers))
        forth(w, (a, up_b) if w % 2 else (a, dn_b)).start()
    for j, (first_row, first_col) in enumerate(((45, 6), (0, 0), (0, 6))):
        send7[j] = piece_of(pack(x_ref, first_row, 3, first_col), pack(g_ref, first_row, 3, first_col))
        forth7(j).start()

    for w in range(7):
        own[w] = both(w, 6 - 6 * (w % 2))

    w_qkv_t[...] = w_qkv[...].T
    w_out_t[...] = w_out[...].T
    head = lax.broadcasted_iota(jnp.int32, (KEYS, 256), 1) // 32
    ones_big[...] = jnp.where(lax.broadcasted_iota(jnp.int32, (KEYS, 256), 0) // TOK == head, 1.0, 0.0).astype(BF)
    head = lax.broadcasted_iota(jnp.int32, (256, KEYS), 0) // 32
    ones_big_t[...] = jnp.where(lax.broadcasted_iota(jnp.int32, (256, KEYS), 1) // TOK == head, 1.0, 0.0).astype(BF)
    head = lax.broadcasted_iota(jnp.int32, (256, 256), 1) // 32
    ones_blk[...] = jnp.where(lax.broadcasted_iota(jnp.int32, (256, 256), 0) // 32 == head, 1.0, 0.0).astype(BF)
    for half in range(2):
        key_head = lax.broadcasted_iota(jnp.int32, (1, KEYS), 1) // TOK
        lane_head = lax.broadcasted_iota(jnp.int32, (1, 256), 1) // 32
        keys = jnp.zeros((1, KEYS), F32)
        lanes = jnp.zeros((1, 256), F32)
        for h in range(8):
            keys = jnp.where(key_head == h, scale_ref[half * 8 + h] * LOG2E, keys)
            lanes = jnp.where(lane_head == h, scale_ref[half * 8 + h], lanes)
        scale_cols[half : half + 1, :] = keys
        scale_lanes[half : half + 1, :] = lanes

    @pl.loop(0, 4)
    def _(pair):
        w = 2 * pair
        forth(w, (a, up_b)).wait_recv()

        @pl.when(pair < 3)
        def _():
            forth(w + 1, (a, up_b)).wait_recv()

        @pl.when(pair == 3)
        def _():
            for j in range(3):
                forth7(j).wait_recv()
            low_x, low_g = pack(x_ref, 45, 3, 0), pack(g_ref, 45, 3, 0)
            side_x, side_g = unpiece(recv7[0])
            down_x, down_g = unpiece(recv7[1])
            diag_x, diag_g = unpiece(recv7[2])
            own[7] = jnp.concatenate([low_x, down_x, low_g, down_g], axis=0).astype(BF)
            recv[7] = jnp.concatenate([side_x, diag_x, side_g, diag_g], axis=0).astype(BF)

        blocks = [ref[w + i].astype(F32) for i in range(2) for ref in (own, recv)]
        xw = jnp.concatenate([block[:HALF] for block in blocks], axis=0).astype(BF)
        gw = jnp.concatenate([block[HALF:] for block in blocks], axis=0)
        split = jnp.logical_and(pair == 3, a == n_lat - 1)
        branch, dshifted, att, dproj, dqkv = pair_math(
            xw,
            gw,
            split,
            w_qkv,
            w_qkv_t,
            w_out,
            w_out_t,
            gain_ref[...],
            scale_cols,
            scale_lanes,
            ones_big,
            ones_big_t,
            ones_blk,
        )
        for i in range(2):
            at = i * TOK
            own_res[w + i] = jnp.concatenate(
                [branch[at : at + HALF], dshifted[at : at + HALF]], axis=0
            ).astype(BF)
            back_send[w + i] = jnp.concatenate(
                [branch[at + HALF : at + TOK], dshifted[at + HALF : at + TOK]], axis=0
            ).astype(BF)
        back(w, (a, up_b)).start()

        @pl.when(pair < 3)
        def _():
            back(w + 1, (a, dn_b)).start()

        rows = pl.ds(pl.multiple_of(pair * 2 * TOK, 2 * TOK), 2 * TOK)
        x_all[rows, :] = xw
        att_all[rows, :] = att
        dproj_all[rows, :] = dproj
        dqkv_all[rows, :] = dqkv

    ours = own_res[7].astype(F32)
    theirs = back_send[7].astype(F32)
    back7_send[0] = piece_of(theirs[:QUART], theirs[HALF : HALF + QUART])
    back7_send[1] = piece_of(ours[QUART:HALF], ours[HALF + QUART :])
    back7_send[2] = piece_of(theirs[QUART:HALF], theirs[HALF + QUART :])
    for j in range(3):
        back7(j).start()

    @pl.loop(0, 2)
    def _(side):
        owner = core * side + (1 - core) * (1 - side)
        at = pl.multiple_of(owner * 768, 256)
        chunks = [tn(x_all[...], dqkv_all[:, pl.ds(at + i * 256, 256)]) for i in range(3)]
        chunks.append(tn(dproj_all[...], att_all[:, pl.ds(pl.multiple_of(owner * 256, 256), 256)]))
        for low in range(2):
            halves = [chunk.reshape(64, 8, 256) for chunk in chunks[2 * low : 2 * low + 2]]
            joined = jnp.concatenate(halves, axis=1).astype(BF)
            for lon in range(64):
                zz, yy, xx = lon // 8, 2 * ((lon // 4) % 2) + low, lon % 4
                uu = xx * (1 - owner) + yy * owner
                vv = yy * (1 - owner) + xx * owner
                grads[side, uu, vv, zz] = joined[lon]

    order = (2, 1, 3, 0)
    pairs = []
    for i, step in enumerate(order):
        c = copy(grads.at[0, mod(v + step, 4)], pair_recv.at[i], pair_send_sem.at[i], pair_recv_sem.at[i], partner)
        c.start()
        pairs.append(c)

    def add_pair(i):
        pairs[i].wait_recv()
        chunk = mod(u + order[i], 4)

        @pl.loop(0, 4)
        def _(vv):
            mine[i, vv] = (grads[1, chunk, vv].astype(F32) + pair_recv[i, vv].astype(F32)).astype(BF)

    def halves_of(w, left):
        came = (w % 2 == 0) == left
        block = (back_recv if came else own_res)[w].astype(F32)
        return block[:HALF], block[HALF:]

    def assemble(lev, left, tops, lows):
        parts = [halves_of(w, left) for w in range(7)]
        for c in range(6):
            at = lev * 6 + c
            for k, (ref, dst) in enumerate(((x_ref, out_ref), (g_ref, gin_ref))):
                strip = (
                    [tops[k][at * 3 : at * 3 + 3]]
                    + [one[k][at * 6 : at * 6 + 6] for one in parts]
                    + [lows[k][at * 3 : at * 3 + 3]]
                )
                cc = c if left else c + 6
                dst[lev, cc] = (ref[lev, cc].astype(F32) + jnp.concatenate(strip, axis=0)).astype(BF)

    add_pair(0)
    relay_up = copy(mine.at[0, pl.ds(0, 2)], ring_relay.at[0], relay_send_sem.at[0], relay_recv_sem.at[0], nxt)
    relay_dn = copy(mine.at[0, pl.ds(2, 2)], ring_relay.at[1], relay_send_sem.at[1], relay_recv_sem.at[1], prv)
    relay_up.start()
    relay_dn.start()
    add_pair(1)
    ring_up_b = copy(mine.at[1, pl.ds(2, 2)], ring_recv.at[0, pl.ds(2, 2)], ring_send_sem.at[0], ring_recv_sem.at[0], nxt)
    ring_up_b.start()
    add_pair(2)
    ring_dn_a = copy(mine.at[2, pl.ds(0, 2)], ring_recv.at[1, pl.ds(0, 2)], ring_send_sem.at[1], ring_recv_sem.at[1], prv)
    ring_dn_a.start()
    add_pair(3)
    relay_up.wait_recv()

    @pl.loop(0, 2)
    def _(vv):
        mine[1, vv] = (mine[1, vv].astype(F32) + ring_relay[0, vv].astype(F32)).astype(BF)

    ring_up_a = copy(mine.at[1, pl.ds(0, 2)], ring_recv.at[0, pl.ds(0, 2)], ring_send_sem.at[2], ring_recv_sem.at[2], nxt)
    ring_up_a.start()
    relay_dn.wait_recv()

    @pl.loop(0, 2)
    def _(vv):
        mine[2, 2 + vv] = (mine[2, 2 + vv].astype(F32) + ring_relay[1, vv].astype(F32)).astype(BF)

    ring_dn_b = copy(mine.at[2, pl.ds(2, 2)], ring_recv.at[1, pl.ds(2, 2)], ring_send_sem.at[3], ring_recv_sem.at[3], prv)
    ring_dn_b.start()

    for w in range(7):
        back(w, (a, up_b)).wait_recv()
    for j in range(3):
        back7(j).wait_recv()
    block = own_res[7].astype(F32)
    near = (block[:QUART], block[HALF : HALF + QUART])
    side, down, diag = (unpiece(back7_recv[j]) for j in range(3))
    assemble(0, True, down, near)
    assemble(0, False, diag, side)

    for c in (ring_up_b, ring_dn_a, ring_up_a, ring_dn_b):
        c.wait_recv()

    @pl.loop(0, 4)
    def _(vv):
        cut[vv] = (
            mine[3, vv].astype(F32) + ring_recv[0, vv].astype(F32) + ring_recv[1, vv].astype(F32)
        ).astype(BF)

    lines = []
    for i in range(3):
        c = copy(cut.at[mod(v + i + 1, 4)], line_recv.at[i], line_send_sem.at[i], line_recv_sem.at[i], line[i])
        c.start()
        lines.append(c)
    assemble(1, True, down, near)
    for c in lines:
        c.wait_recv()
    piece[...] = (
        cut[v].astype(F32) + line_recv[0].astype(F32) + line_recv[1].astype(F32) + line_recv[2].astype(F32)
    ).astype(BF)
    columns = []
    for i in range(7):
        c = copy(piece.at[mod(z + i + 1, 8)], z_recv.at[i], z_send_sem.at[i], z_recv_sem.at[i], column[i])
        c.start()
        columns.append(c)
    assemble(1, False, diag, side)
    for c in columns:
        c.wait_recv()
    total = piece[z].astype(F32)
    for i in range(7):
        total = total + z_recv[i].astype(F32)
    part[...] = total

    here = 2 * core + y_lo
    whole[here] = total
    gathers = []
    for i in range(3):
        c = copy(part, whole.at[here], gather_send_sem.at[i], gather_recv_sem.at[i], group[i])
        c.start()
        gathers.append(c)

    for w in range(7):
        forth(w, (a, up_b)).wait_send()
        back(w, (a, up_b)).wait_send()
    for j in range(3):
        forth7(j).wait_send()
        back7(j).wait_send()
    for c in pairs + [relay_up, relay_dn, ring_up_b, ring_dn_a, ring_up_a, ring_dn_b] + lines + columns:
        c.wait_send()
    for c in gathers:
        c.wait_recv()
    for owner in range(2):
        at = owner * 768
        gq_ref[:, at : at + 256] = whole[2 * owner, 0:8, :]
        gq_ref[:, at + 256 : at + 512] = whole[2 * owner, 8:16, :]
        gq_ref[:, at + 512 : at + 768] = whole[2 * owner + 1, 0:8, :]
        go_ref[:, owner * 256 : owner * 256 + 256] = whole[2 * owner + 1, 8:16, :]
    for c in gathers:
        c.wait_send()


def body(inputs, cotangent, w_qkv, w_out, gain, logit_scale):
    vmem = pl.BlockSpec(memory_space=pltpu.VMEM)
    smem = pl.BlockSpec(memory_space=pltpu.SMEM)
    dma = pltpu.SemaphoreType.DMA
    blocks = pltpu.VMEM((8, TOK, WIDTH), BF)
    pieces = pltpu.VMEM((3, 80, WIDTH), BF)
    x_view = inputs.transpose(0, 2, 1, 3)
    g_view = cotangent.transpose(0, 2, 1, 3)
    out, grad_in, share_qkv, share_out = pl.pallas_call(
        block_kernel,
        out_shape=[
            jax.ShapeDtypeStruct(x_view.shape, BF),
            jax.ShapeDtypeStruct(x_view.shape, BF),
            jax.ShapeDtypeStruct((8, 3 * WIDTH), F32),
            jax.ShapeDtypeStruct((8, WIDTH), F32),
        ],
        in_specs=[vmem] * 5 + [smem],
        out_specs=[vmem] * 4,
        scratch_shapes=[blocks] * 6
        + [pieces] * 4
        + [
            pltpu.VMEM((8 * TOK, WIDTH), BF),
            pltpu.VMEM((8 * TOK, WIDTH), BF),
            pltpu.VMEM((8 * TOK, WIDTH), BF),
            pltpu.VMEM((8 * TOK, 3 * WIDTH), BF),
            pltpu.VMEM((3 * WIDTH, WIDTH), BF),
            pltpu.VMEM((WIDTH, WIDTH), BF),
            pltpu.VMEM((KEYS, 256), BF),
            pltpu.VMEM((256, KEYS), BF),
            pltpu.VMEM((256, 256), BF),
            pltpu.VMEM((2, KEYS), F32),
            pltpu.VMEM((2, 256), F32),
            pltpu.VMEM((2, 4, 4, 8, 16, 256), BF),
            pltpu.VMEM((4, 4, 8, 16, 256), BF),
            pltpu.VMEM((4, 4, 8, 16, 256), BF),
            pltpu.VMEM((2, 2, 8, 16, 256), BF),
            pltpu.VMEM((2, 4, 8, 16, 256), BF),
            pltpu.VMEM((4, 8, 16, 256), BF),
            pltpu.VMEM((3, 8, 16, 256), BF),
            pltpu.VMEM((8, 16, 256), BF),
            pltpu.VMEM((7, 16, 256), BF),
            pltpu.VMEM((16, 256), F32),
            pltpu.VMEM((4, 16, 256), F32),
        ]
        + [dma((7,))] * 4
        + [dma((3,))] * 4
        + [dma((4,))] * 2
        + [dma((2,))] * 2
        + [dma((4,))] * 2
        + [dma((3,))] * 2
        + [dma((7,))] * 2
        + [dma((3,))] * 2,
        compiler_params=pltpu.CompilerParams(
            collective_id=0, has_side_effects=True, vmem_limit_bytes=56 * 2**20
        ),
    )(x_view, g_view, w_qkv, w_out, gain.reshape(1, WIDTH), logit_scale)
    return out.transpose(0, 2, 1, 3), grad_in.transpose(0, 2, 1, 3), share_qkv, share_out.T


def solution(mesh):
    placed = (P(None, "lat", "lon", None), P(None, "lat", "lon", None), P(), P(), P(), P())
    return jax.shard_map(
        body,
        mesh=mesh,
        in_specs=placed,
        out_specs=(
            P(None, "lat", "lon", None),
            P(None, "lat", "lon", None),
            P("lon", None),
            P(None, "lon"),
        ),
        check_vma=False,
    )
```

```python
import jax
import jax.numpy as jnp
from jax import lax
from jax.experimental import pallas as pl
from jax.experimental.pallas import tpu as pltpu
from jax.sharding import PartitionSpec as P

BF = jnp.bfloat16
F32 = jnp.float32
MESH = pl.DeviceIdType.MESH
HEADS = 16
WIDTH = 512
HALF = 72
TOK = 144
QUART = 36
KEYS = 8 * TOK
LOG2E = 1.4426950408889634
FLOOR = 1e-6
EPS = 1e-5


def nn(a, b):
    return jnp.dot(a, b, preferred_element_type=F32)


def nt(a, b):
    return lax.dot_general(a, b, (((1,), (1,)), ((), ())), preferred_element_type=F32)


def tn(a, b):
    return lax.dot_general(a, b, (((0,), (0,)), ((), ())), preferred_element_type=F32)


def key_head(place):
    return jnp.where(place < 1024, place // 128, (place - 1024) // 16)


def key_token(place):
    return jnp.where(place < 1024, place % 128, 128 + (place - 1024) % 16)


def spread(part):
    head = lax.broadcasted_iota(jnp.int32, part.shape, 1) // 32
    zero = jnp.zeros_like(part)
    alone = [jnp.where(head == h, part, zero) for h in range(8)]
    return jnp.concatenate([one[:128] for one in alone] + [one[128:] for one in alone], axis=0)


def spread_t(part):
    main = part[:128].T
    row = lax.broadcasted_iota(jnp.int32, main.shape, 0) // 32
    zero = jnp.zeros_like(main)
    rest = part[128:]
    head = lax.broadcasted_iota(jnp.int32, rest.shape, 1) // 32
    last = jnp.concatenate([jnp.where(head == h, rest, jnp.zeros_like(rest)) for h in range(8)], axis=0).T
    return jnp.concatenate([jnp.where(row == h, main, zero) for h in range(8)] + [last], axis=1)


def pick(full):
    def choose(first, step, rows):
        head = lax.broadcasted_iota(jnp.int32, (rows, 256), 1) // 32
        chosen = full[first : first + rows]
        for h in range(1, 8):
            chosen = jnp.where(head == h, full[first + step * h : first + step * h + rows], chosen)
        return chosen

    return jnp.concatenate([choose(0, 128, 128), choose(1024, 16, 16)], axis=0)


def head_sum(value, ones_block):
    return nn(value.astype(BF), ones_block)


def head_sum_fine(value, ones_block):
    high = value.astype(BF)
    low = (value - high.astype(F32)).astype(BF)
    return nn(high, ones_block) + nn(low, ones_block)


def pair_math(x, wait_gw, split, w_qkv, w_out, w_out_t, gain, scale_cols, scale_lanes, ones_big, minus_ones_t, ones_blk):
    ones_block = ones_blk[...]
    qkv = nn(x, w_qkv[...]).astype(BF)
    row = lax.broadcasted_iota(jnp.int32, (TOK, 1), 0)
    col = key_token(lax.broadcasted_iota(jnp.int32, (1, KEYS), 1))
    allowed = jnp.where(split, (row // QUART) % 2, 0) == jnp.where(split, (col // QUART) % 2, 0)
    vec = []
    for half in range(2):
        lo = half * 256
        q = qkv[:, lo : lo + 256].astype(F32)
        k = qkv[:, 512 + lo : 768 + lo].astype(F32)
        q_len = jnp.sqrt(head_sum_fine(q * q, ones_block))
        k_len = jnp.sqrt(head_sum_fine(k * k, ones_block))
        q_inv = 1.0 / jnp.maximum(q_len, FLOOR)
        k_inv = 1.0 / jnp.maximum(k_len, FLOOR)
        uq = q * q_inv
        uk = k * k_inv
        vec.append((q_len, k_len, q_inv, k_inv, uq, uk, uq.astype(BF), uk.astype(BF)))
    att = [[None, None], [None, None]]
    saved = {}
    for g in range(2):
        r = slice(g * TOK, (g + 1) * TOK)
        for half in range(2):
            lo = half * 256
            uq, uk = vec[half][6][r], vec[half][7][r]
            k_big = spread(uk)
            v = qkv[r, 1024 + lo : 1280 + lo]
            v_big = spread(v)
            e = jnp.exp2(nn(uq, spread_t(uk)) * scale_cols[half : half + 1, :])
            if g == 1:
                e = jnp.where(allowed, e, 0.0)
            e = e.astype(BF)
            both = nn(e, jnp.concatenate([v_big, ones_big[...]], axis=1))
            r_den = 1.0 / both[:, 256:]
            att[g][half] = (both[:, :256] * r_den).astype(BF)
            saved[g, half] = (k_big, v, e, r_den, uq)
    att_b = jnp.concatenate([jnp.concatenate(one, axis=1) for one in att], axis=0)
    proj = nn(att_b, w_out[...])
    dev = proj - jnp.mean(proj, -1, keepdims=True)
    inv = lax.rsqrt(jnp.mean(dev * dev, -1, keepdims=True) + EPS)
    normed = dev * inv
    branch = gain * normed
    up = gain * wait_gw()
    dproj = (
        (up - jnp.mean(up, -1, keepdims=True) - normed * jnp.mean(up * normed, -1, keepdims=True))
        * inv
    ).astype(BF)
    datt = nn(dproj, w_out_t[...]).astype(BF)
    dq, dk, dv = {}, {}, {}
    for g in range(2):
        r = slice(g * TOK, (g + 1) * TOK)
        for half in range(2):
            lo = half * 256
            k_big, v, e, r_den, uq = saved[g, half]
            dh = datt[r, lo : lo + 256].astype(F32) * r_den
            dh_b = dh.astype(BF)
            dd = (dh * att[g][half].astype(F32)).astype(BF)
            t = nn(
                jnp.concatenate([dh_b, dd], axis=1),
                jnp.concatenate([spread_t(v), minus_ones_t[...]], axis=0),
            )
            ds = (e.astype(F32) * t).astype(BF)
            lanes = scale_lanes[half : half + 1, :]
            dq[g, half] = nn(ds, k_big) * lanes
            dk[g, half] = pick(tn(ds, uq)) * lanes
            dv[g, half] = pick(tn(e, dh_b)).astype(BF)
    cols = [None] * 6
    for half in range(2):
        q_len, k_len, q_inv, k_inv, uq, uk, _, _ = vec[half]
        duq = jnp.concatenate([dq[0, half], dq[1, half]], axis=0)
        duk = jnp.concatenate([dk[0, half], dk[1, half]], axis=0)
        q_tail = jnp.where(q_len > FLOOR, uq * head_sum(uq * duq, ones_block), 0.0)
        k_tail = jnp.where(k_len > FLOOR, uk * head_sum(uk * duk, ones_block), 0.0)
        cols[half] = ((duq - q_tail) * q_inv).astype(BF)
        cols[2 + half] = ((duk - k_tail) * k_inv).astype(BF)
        cols[4 + half] = jnp.concatenate([dv[0, half], dv[1, half]], axis=0)
    dqkv = jnp.concatenate(cols, axis=1)
    return branch, att_b, dproj, dqkv


def pack(ref, first_row, rows, first_col):
    low = first_row // 16 * 16
    high = (first_row + rows + 15) // 16 * 16
    parts = []
    for lev in range(2):
        for c in range(first_col, first_col + 6):
            strip = ref[lev, c, low:high, :].astype(F32)
            parts.append(strip[first_row - low : first_row - low + rows])
    return jnp.concatenate(parts, axis=0)


def padded(part):
    return jnp.concatenate([part, jnp.zeros((8, WIDTH), F32)], axis=0).astype(BF)


def piece_of(x_part, g_part):
    pad = jnp.zeros((4, WIDTH), F32)
    return jnp.concatenate([x_part, pad, g_part, pad], axis=0).astype(BF)


def unpiece(ref):
    whole = ref.astype(F32)
    return whole[:QUART], whole[40 : 40 + QUART]


def block_kernel(
    x_hbm,
    g_hbm,
    w_qkv_hbm,
    w_out_hbm,
    gain_ref,
    scale_ref,
    out_hbm,
    gin_hbm,
    gq_ref,
    go_ref,
    x_ref,
    g_ref,
    w_qkv,
    w_out,
    out_ref,
    gin_ref,
    send,
    recv,
    own,
    back_send,
    back_recv,
    own_res,
    send7,
    recv7,
    back7_send,
    back7_recv,
    x_all,
    att_all,
    dproj_all,
    dqkv_all,
    w_qkv_t,
    w_out_t,
    ones_big,
    minus_ones_t,
    ones_blk,
    scale_cols,
    scale_lanes,
    grads,
    pair_recv,
    mine,
    ring_relay,
    ring_recv,
    cut,
    line_recv,
    piece,
    z_recv,
    part,
    whole,
    send_sem,
    recv_sem,
    back_send_sem,
    back_recv_sem,
    send7_sem,
    recv7_sem,
    back7_send_sem,
    back7_recv_sem,
    pair_send_sem,
    pair_recv_sem,
    relay_send_sem,
    relay_recv_sem,
    ring_send_sem,
    ring_recv_sem,
    line_send_sem,
    line_recv_sem,
    z_send_sem,
    z_recv_sem,
    gather_send_sem,
    gather_recv_sem,
    load_sem,
    store_sem,
):
    loads = [
        pltpu.make_async_copy(src, dst, load_sem.at[i])
        for i, (src, dst) in enumerate(((x_hbm, x_ref), (g_hbm, g_ref), (w_qkv_hbm, w_qkv), (w_out_hbm, w_out)))
    ]
    for c in loads:
        c.start()
    n_lat = lax.axis_size("lat")
    n_lon = lax.axis_size("lon")
    a = lax.axis_index("lat")
    b = lax.axis_index("lon")

    def mod(value, n):
        return lax.rem(value + n, n)

    up_a, dn_a = mod(a + 1, n_lat), mod(a - 1, n_lat)
    up_b, dn_b = mod(b + 1, n_lon), mod(b - 1, n_lon)
    core, y_lo = lax.rem(a, 2), a // 2
    z, y_hi, x = b // 8, lax.rem(b // 4, 2), lax.rem(b, 4)
    y = 2 * y_hi + y_lo
    u = x * (1 - core) + y * core
    v = y * (1 - core) + x * core

    def device(uu, vv, zz):
        xx = uu * (1 - core) + vv * core
        yy = vv * (1 - core) + uu * core
        return (2 * lax.rem(yy, 2) + core, zz * 8 + (yy // 2) * 4 + xx)

    partner = (a + 1 - 2 * core, b)
    nxt = device(mod(u + 1, 4), v, z)
    prv = device(mod(u + 3, 4), v, z)
    line = [device(u, mod(v + i, 4), z) for i in range(1, 4)]
    column = [device(u, v, mod(z + i, 8)) for i in range(1, 8)]
    group = [(mod(a + i, 4), b) for i in range(1, 4)]
    around = [(a, up_b), (a, dn_b), (up_a, b), (dn_a, b), (up_a, dn_b), (dn_a, up_b)]
    peers = around + [partner, nxt, prv] + line + column + group

    barrier = pltpu.get_barrier_semaphore()
    for peer in peers:
        pl.semaphore_signal(barrier, inc=1, device_id=peer, device_id_type=MESH)

    def copy(src, dst, send_sem, recv_sem, peer):
        return pltpu.make_async_remote_copy(
            src_ref=src, dst_ref=dst, send_sem=send_sem, recv_sem=recv_sem, device_id=peer, device_id_type=MESH
        )

    def forth(w, k, peer):
        return copy(send.at[w, k], recv.at[w, k], send_sem.at[w, k], recv_sem.at[w, k], peer)

    def back(w, peer):
        return copy(back_send.at[w], back_recv.at[w], back_send_sem.at[w], back_recv_sem.at[w], peer)

    def forth7(j):
        peer = ((a, up_b), (dn_a, b), (dn_a, up_b))[j]
        return copy(send7.at[j], recv7.at[j], send7_sem.at[j], recv7_sem.at[j], peer)

    def back7(j):
        peer = ((a, dn_b), (up_a, b), (up_a, dn_b))[j]
        return copy(back7_send.at[j], back7_recv.at[j], back7_send_sem.at[j], back7_recv_sem.at[j], peer)

    loads[0].wait()
    for w in range(2):
        send[w, 0] = padded(pack(x_ref, 6 * w + 3, 6, 6 * (w % 2)))
    loads[1].wait()
    for w in range(2):
        send[w, 1] = padded(pack(g_ref, 6 * w + 3, 6, 6 * (w % 2)))
    pl.semaphore_wait(barrier, len(peers))
    for k in range(2):
        for w in range(2):
            forth(w, k, (a, up_b) if w % 2 else (a, dn_b)).start()
    for w in range(2, 7):
        for k, ref in enumerate((x_ref, g_ref)):
            send[w, k] = padded(pack(ref, 6 * w + 3, 6, 6 * (w % 2)))
            forth(w, k, (a, up_b) if w % 2 else (a, dn_b)).start()
    for j, (first_row, first_col) in enumerate(((45, 6), (0, 0), (0, 6))):
        send7[j] = piece_of(pack(x_ref, first_row, 3, first_col), pack(g_ref, first_row, 3, first_col))
        forth7(j).start()

    for w in range(7):
        for k, ref in enumerate((x_ref, g_ref)):
            own[w, k] = padded(pack(ref, 6 * w + 3, 6, 6 - 6 * (w % 2)))

    loads[2].wait()
    loads[3].wait()
    w_qkv_t[...] = w_qkv[...].T
    w_out_t[...] = w_out[...].T
    head = lax.broadcasted_iota(jnp.int32, (KEYS, 256), 1) // 32
    place = key_head(lax.broadcasted_iota(jnp.int32, (KEYS, 256), 0))
    ones_big[...] = jnp.where(place == head, 1.0, 0.0).astype(BF)
    head = lax.broadcasted_iota(jnp.int32, (256, KEYS), 0) // 32
    place = key_head(lax.broadcasted_iota(jnp.int32, (256, KEYS), 1))
    minus_ones_t[...] = jnp.where(place == head, -1.0, 0.0).astype(BF)
    head = lax.broadcasted_iota(jnp.int32, (256, 256), 1) // 32
    ones_blk[...] = jnp.where(lax.broadcasted_iota(jnp.int32, (256, 256), 0) // 32 == head, 1.0, 0.0).astype(BF)
    for half in range(2):
        col_head = key_head(lax.broadcasted_iota(jnp.int32, (1, KEYS), 1))
        lane_head = lax.broadcasted_iota(jnp.int32, (1, 256), 1) // 32
        keys = jnp.zeros((1, KEYS), F32)
        lanes = jnp.zeros((1, 256), F32)
        for h in range(8):
            keys = jnp.where(col_head == h, scale_ref[half * 8 + h] * LOG2E, keys)
            lanes = jnp.where(lane_head == h, scale_ref[half * 8 + h], lanes)
        scale_cols[half : half + 1, :] = keys
        scale_lanes[half : half + 1, :] = lanes

    def results(w, part, branch, dshifted):
        at = part * TOK
        if branch is not None:
            own_res[w, 0:HALF] = branch[at : at + HALF].astype(BF)
            back_send[w, 0:HALF] = branch[at + HALF : at + TOK].astype(BF)
        if dshifted is not None:
            own_res[w, 80 : 80 + HALF] = dshifted[at : at + HALF].astype(BF)
            back_send[w, 80 : 80 + HALF] = dshifted[at + HALF : at + TOK].astype(BF)

    for w in range(8):
        for row in (HALF, 80 + HALF):
            back_send[w, row : row + 8] = jnp.zeros((8, WIDTH), BF)

    @pl.loop(0, 4)
    def _(pair):
        w = 2 * pair
        forth(w, 0, (a, up_b)).wait_recv()

        @pl.when(pair < 3)
        def _():
            forth(w + 1, 0, (a, up_b)).wait_recv()

        @pl.when(pair == 3)
        def _():
            for j in range(3):
                forth7(j).wait_recv()
            low = pack(x_ref, 45, 3, 0), pack(g_ref, 45, 3, 0)
            side, down, diag = (unpiece(recv7[j]) for j in range(3))
            for k in range(2):
                own[7, k] = padded(jnp.concatenate([low[k], down[k]], axis=0))
                recv[7, k] = padded(jnp.concatenate([side[k], diag[k]], axis=0))

        def tokens(k):
            blocks = [ref[w + i, k].astype(F32)[:HALF] for i in range(2) for ref in (own, recv)]
            return jnp.concatenate(blocks, axis=0)

        def wait_gw():
            forth(w, 1, (a, up_b)).wait_recv()

            @pl.when(pair < 3)
            def _():
                forth(w + 1, 1, (a, up_b)).wait_recv()

            return tokens(1)

        xw = tokens(0).astype(BF)
        split = jnp.logical_and(pair == 3, a == n_lat - 1)
        branch, att, dproj, dqkv = pair_math(
            xw,
            wait_gw,
            split,
            w_qkv,
            w_out,
            w_out_t,
            gain_ref[...],
            scale_cols,
            scale_lanes,
            ones_big,
            minus_ones_t,
            ones_blk,
        )
        for i in range(2):
            results(w + i, i, branch, None)
        rows = pl.ds(pl.multiple_of(pair * 2 * TOK, 2 * TOK), 2 * TOK)
        x_all[rows, :] = xw
        att_all[rows, :] = att
        dproj_all[rows, :] = dproj
        dqkv_all[rows, :] = dqkv

        @pl.when(pair < 3)
        def _():
            dshifted = nn(dqkv_all[rows, :], w_qkv_t[...])
            for i in range(2):
                results(w + i, i, None, dshifted)
            back(w, (a, up_b)).start()
            back(w + 1, (a, dn_b)).start()

    def columns_of(owner, side):
        at = pl.multiple_of(owner * 768, 256)
        chunks = [tn(x_all[...], dqkv_all[:, pl.ds(at + i * 256, 256)]) for i in range(3)]
        chunks.append(tn(dproj_all[...], att_all[:, pl.ds(pl.multiple_of(owner * 256, 256), 256)]))
        for low in range(2):
            halves = [chunk.reshape(64, 8, 256) for chunk in chunks[2 * low : 2 * low + 2]]
            joined = jnp.concatenate(halves, axis=1).astype(BF)
            for lon in range(64):
                zz, yy, xx = lon // 8, 2 * ((lon // 4) % 2) + low, lon % 4
                uu = xx * (1 - owner) + yy * owner
                vv = yy * (1 - owner) + xx * owner
                grads[side, uu, vv, zz] = joined[lon]

    columns_of(1 - core, 0)

    order = (2, 1, 3, 0)
    pairs = []
    for i, step in enumerate(order):
        c = copy(grads.at[0, mod(v + step, 4)], pair_recv.at[i], pair_send_sem.at[i], pair_recv_sem.at[i], partner)
        c.start()
        pairs.append(c)

    columns_of(core, 1)
    dshifted = nn(dqkv_all[6 * TOK :, :], w_qkv_t[...])
    for i in range(2):
        results(6 + i, i, None, dshifted)
    back(6, (a, up_b)).start()
    ours = own_res[7].astype(F32)
    theirs = back_send[7].astype(F32)
    back7_send[0] = piece_of(theirs[:QUART], theirs[80 : 80 + QUART])
    back7_send[1] = piece_of(ours[QUART:HALF], ours[80 + QUART : 80 + HALF])
    back7_send[2] = piece_of(theirs[QUART:HALF], theirs[80 + QUART : 80 + HALF])
    for j in range(3):
        back7(j).start()

    def add_pair(i):
        pairs[i].wait_recv()
        chunk = mod(u + order[i], 4)

        @pl.loop(0, 4)
        def _(vv):
            mine[i, vv] = (grads[1, chunk, vv].astype(F32) + pair_recv[i, vv].astype(F32)).astype(BF)

    def halves_of(w, left):
        came = (w % 2 == 0) == left
        block = (back_recv if came else own_res)[w].astype(F32)
        return block[:HALF], block[80 : 80 + HALF]

    def assemble(lev, left, tops, lows):
        parts = [halves_of(w, left) for w in range(7)]
        for c in range(6):
            at = lev * 6 + c
            for k, (ref, dst) in enumerate(((x_ref, out_ref), (g_ref, gin_ref))):
                strip = (
                    [tops[k][at * 3 : at * 3 + 3]]
                    + [one[k][at * 6 : at * 6 + 6] for one in parts]
                    + [lows[k][at * 3 : at * 3 + 3]]
                )
                cc = c if left else c + 6
                dst[lev, cc] = (ref[lev, cc].astype(F32) + jnp.concatenate(strip, axis=0)).astype(BF)
        place = pl.ds(0 if left else 6, 6)
        for k, (src, dst) in enumerate(((out_ref, out_hbm), (gin_ref, gin_hbm))):
            i = (2 * lev + (0 if left else 1)) * 2 + k
            c = pltpu.make_async_copy(src.at[lev, place], dst.at[lev, place], store_sem.at[i])
            c.start()
            stores.append(c)

    stores = []

    add_pair(0)
    relay_up = copy(mine.at[0, pl.ds(0, 2)], ring_relay.at[0], relay_send_sem.at[0], relay_recv_sem.at[0], nxt)
    relay_dn = copy(mine.at[0, pl.ds(2, 2)], ring_relay.at[1], relay_send_sem.at[1], relay_recv_sem.at[1], prv)
    relay_up.start()
    relay_dn.start()
    add_pair(1)
    ring_up_b = copy(mine.at[1, pl.ds(2, 2)], ring_recv.at[0, pl.ds(2, 2)], ring_send_sem.at[0], ring_recv_sem.at[0], nxt)
    ring_up_b.start()
    add_pair(2)
    ring_dn_a = copy(mine.at[2, pl.ds(0, 2)], ring_recv.at[1, pl.ds(0, 2)], ring_send_sem.at[1], ring_recv_sem.at[1], prv)
    ring_dn_a.start()
    add_pair(3)
    relay_up.wait_recv()

    @pl.loop(0, 2)
    def _(vv):
        mine[1, vv] = (mine[1, vv].astype(F32) + ring_relay[0, vv].astype(F32)).astype(BF)

    ring_up_a = copy(mine.at[1, pl.ds(0, 2)], ring_recv.at[0, pl.ds(0, 2)], ring_send_sem.at[2], ring_recv_sem.at[2], nxt)
    ring_up_a.start()
    relay_dn.wait_recv()

    @pl.loop(0, 2)
    def _(vv):
        mine[2, 2 + vv] = (mine[2, 2 + vv].astype(F32) + ring_relay[1, vv].astype(F32)).astype(BF)

    ring_dn_b = copy(mine.at[2, pl.ds(2, 2)], ring_recv.at[1, pl.ds(2, 2)], ring_send_sem.at[3], ring_recv_sem.at[3], prv)
    ring_dn_b.start()

    for w in range(7):
        back(w, (a, up_b)).wait_recv()
    for j in range(3):
        back7(j).wait_recv()
    block = own_res[7].astype(F32)
    near = (block[:QUART], block[80 : 80 + QUART])
    side, down, diag = (unpiece(back7_recv[j]) for j in range(3))
    assemble(0, True, down, near)
    assemble(0, False, diag, side)

    for c in (ring_up_b, ring_dn_a, ring_up_a, ring_dn_b):
        c.wait_recv()

    @pl.loop(0, 4)
    def _(vv):
        cut[vv] = (
            mine[3, vv].astype(F32) + ring_recv[0, vv].astype(F32) + ring_recv[1, vv].astype(F32)
        ).astype(BF)

    lines = []
    for i in range(3):
        c = copy(cut.at[mod(v + i + 1, 4)], line_recv.at[i], line_send_sem.at[i], line_recv_sem.at[i], line[i])
        c.start()
        lines.append(c)
    assemble(1, True, down, near)
    for c in lines:
        c.wait_recv()
    piece[...] = (
        cut[v].astype(F32) + line_recv[0].astype(F32) + line_recv[1].astype(F32) + line_recv[2].astype(F32)
    ).astype(BF)
    columns = []
    for i in range(7):
        c = copy(piece.at[mod(z + i + 1, 8)], z_recv.at[i], z_send_sem.at[i], z_recv_sem.at[i], column[i])
        c.start()
        columns.append(c)
    assemble(1, False, diag, side)
    for c in columns:
        c.wait_recv()
    total = piece[z].astype(F32)
    for i in range(7):
        total = total + z_recv[i].astype(F32)
    part[...] = total

    here = 2 * core + y_lo
    whole[here] = total
    gathers = []
    for i in range(3):
        c = copy(part, whole.at[here], gather_send_sem.at[i], gather_recv_sem.at[i], group[i])
        c.start()
        gathers.append(c)

    for w in range(7):
        for k in range(2):
            forth(w, k, (a, up_b)).wait_send()
        back(w, (a, up_b)).wait_send()
    for j in range(3):
        forth7(j).wait_send()
        back7(j).wait_send()
    for c in pairs + [relay_up, relay_dn, ring_up_b, ring_dn_a, ring_up_a, ring_dn_b] + lines + columns:
        c.wait_send()
    for c in gathers:
        c.wait_recv()
    for owner in range(2):
        at = owner * 768
        gq_ref[:, at : at + 256] = whole[2 * owner, 0:8, :]
        gq_ref[:, at + 256 : at + 512] = whole[2 * owner, 8:16, :]
        gq_ref[:, at + 512 : at + 768] = whole[2 * owner + 1, 0:8, :]
        go_ref[:, owner * 256 : owner * 256 + 256] = whole[2 * owner + 1, 8:16, :]
    for c in gathers:
        c.wait_send()
    for c in stores:
        c.wait()


def move_kernel(*refs):
    sources, targets, held, in_sem, out_sem = refs[:4], refs[4:8], refs[8:12], refs[12], refs[13]
    moves = []
    for i in range(4):
        for part in range(2) if i < 2 else (0,):
            n = len(moves)
            views = [ref.at[part] if i < 2 else ref for ref in (sources[i], held[i], targets[i])]
            first = pltpu.make_async_copy(views[0], views[1], in_sem.at[n])
            second = pltpu.make_async_copy(views[1], views[2], out_sem.at[n])
            first.start()
            moves.append((first, second))
    for first, second in moves:
        first.wait()
        second.start()
    for first, second in moves:
        second.wait()


def body(inputs, cotangent, w_qkv, w_out, gain, logit_scale):
    vmem = pl.BlockSpec(memory_space=pltpu.VMEM)
    smem = pl.BlockSpec(memory_space=pltpu.SMEM)
    dma = pltpu.SemaphoreType.DMA
    anywhere = pl.BlockSpec(memory_space=pl.ANY)
    halves = pltpu.VMEM((8, 2, 80, WIDTH), BF)
    blocks = pltpu.VMEM((8, 160, WIDTH), BF)
    pieces = pltpu.VMEM((3, 80, WIDTH), BF)
    x_view = inputs.transpose(0, 2, 1, 3)
    g_view = cotangent.transpose(0, 2, 1, 3)
    out, grad_in, share_qkv, share_out = pl.pallas_call(
        block_kernel,
        out_shape=[
            jax.ShapeDtypeStruct(x_view.shape, BF),
            jax.ShapeDtypeStruct(x_view.shape, BF),
            jax.ShapeDtypeStruct((8, 3 * WIDTH), F32),
            jax.ShapeDtypeStruct((8, WIDTH), F32),
        ],
        in_specs=[anywhere] * 4 + [vmem, smem],
        out_specs=[anywhere] * 2 + [vmem] * 2,
        scratch_shapes=[
            pltpu.VMEM(x_view.shape, BF),
            pltpu.VMEM(x_view.shape, BF),
            pltpu.VMEM(w_qkv.shape, BF),
            pltpu.VMEM(w_out.shape, BF),
            pltpu.VMEM(x_view.shape, BF),
            pltpu.VMEM(x_view.shape, BF),
        ]
        + [halves] * 3
        + [blocks] * 3
        + [pieces] * 4
        + [
            pltpu.VMEM((8 * TOK, WIDTH), BF),
            pltpu.VMEM((8 * TOK, WIDTH), BF),
            pltpu.VMEM((8 * TOK, WIDTH), BF),
            pltpu.VMEM((8 * TOK, 3 * WIDTH), BF),
            pltpu.VMEM((3 * WIDTH, WIDTH), BF),
            pltpu.VMEM((WIDTH, WIDTH), BF),
            pltpu.VMEM((KEYS, 256), BF),
            pltpu.VMEM((256, KEYS), BF),
            pltpu.VMEM((256, 256), BF),
            pltpu.VMEM((2, KEYS), F32),
            pltpu.VMEM((2, 256), F32),
            pltpu.VMEM((2, 4, 4, 8, 16, 256), BF),
            pltpu.VMEM((4, 4, 8, 16, 256), BF),
            pltpu.VMEM((4, 4, 8, 16, 256), BF),
            pltpu.VMEM((2, 2, 8, 16, 256), BF),
            pltpu.VMEM((2, 4, 8, 16, 256), BF),
            pltpu.VMEM((4, 8, 16, 256), BF),
            pltpu.VMEM((3, 8, 16, 256), BF),
            pltpu.VMEM((8, 16, 256), BF),
            pltpu.VMEM((7, 16, 256), BF),
            pltpu.VMEM((16, 256), F32),
            pltpu.VMEM((4, 16, 256), F32),
        ]
        + [dma((7, 2))] * 2
        + [dma((7,))] * 2
        + [dma((3,))] * 4
        + [dma((4,))] * 2
        + [dma((2,))] * 2
        + [dma((4,))] * 2
        + [dma((3,))] * 2
        + [dma((7,))] * 2
        + [dma((3,))] * 2
        + [dma((4,)), dma((8,))],
        compiler_params=pltpu.CompilerParams(
            collective_id=0, has_side_effects=True, vmem_limit_bytes=56 * 2**20
        ),
    )(x_view, g_view, w_qkv, w_out, gain.reshape(1, WIDTH), logit_scale)
    results = (out, grad_in, share_qkv, share_out)
    out, grad_in, share_qkv, share_out = pl.pallas_call(
        move_kernel,
        out_shape=[jax.ShapeDtypeStruct(r.shape, r.dtype) for r in results],
        in_specs=[anywhere] * 4,
        out_specs=[anywhere] * 4,
        scratch_shapes=[pltpu.VMEM(r.shape, r.dtype) for r in results] + [dma((6,)), dma((6,))],
    )(*results)
    return out.transpose(0, 2, 1, 3), grad_in.transpose(0, 2, 1, 3), share_qkv, share_out.T


def solution(mesh):
    placed = (P(None, "lat", "lon", None), P(None, "lat", "lon", None), P(), P(), P(), P())
    return jax.shard_map(
        body,
        mesh=mesh,
        in_specs=placed,
        out_specs=(
            P(None, "lat", "lon", None),
            P(None, "lat", "lon", None),
            P("lon", None),
            P(None, "lon"),
        ),
        check_vma=False,
    )
```

```python
import jax
import jax.numpy as jnp
from jax import lax
from jax.experimental import pallas as pl
from jax.experimental.pallas import tpu as pltpu
from jax.sharding import PartitionSpec as P

BF = jnp.bfloat16
F32 = jnp.float32
MESH = pl.DeviceIdType.MESH
HEADS = 16
WIDTH = 512
HALF = 72
TOK = 144
QUART = 36
KEYS = 8 * TOK
LOG2E = 1.4426950408889634
FLOOR = 1e-6
EPS = 1e-5


def nn(a, b):
    return jnp.dot(a, b, preferred_element_type=F32)


def nt(a, b):
    return lax.dot_general(a, b, (((1,), (1,)), ((), ())), preferred_element_type=F32)


def tn(a, b):
    return lax.dot_general(a, b, (((0,), (0,)), ((), ())), preferred_element_type=F32)


def key_head(place):
    return jnp.where(place < 1024, place // 128, (place - 1024) // 16)


def key_token(place):
    return jnp.where(place < 1024, place % 128, 128 + (place - 1024) % 16)


def alone(part, axis, heads):
    head = lax.broadcasted_iota(jnp.int32, part.shape, axis) // 32
    zero = jnp.zeros_like(part)
    return [jnp.where(head == h, part, zero) for h in range(heads)]


def rows4(part, p):
    return jnp.concatenate(alone(part[:128, 128 * p : 128 * p + 128], 1, 4), axis=0)


def rows_last(part):
    return jnp.concatenate(alone(part[128:], 1, 8), axis=0)


def cols4(main_t, p):
    return jnp.concatenate(alone(main_t[128 * p : 128 * p + 128], 0, 4), axis=1)


def by_keys(e, d):
    d_t = d.T
    blocks = []
    for p in range(4):
        two = nn(d_t[64 * p : 64 * p + 64], e[:, 256 * p : 256 * p + 256])
        blocks += [two[:32, :128], two[32:, 128:]]
    full = tn(e[:, 1024:], d)
    head = lax.broadcasted_iota(jnp.int32, (16, 256), 1) // 32
    last = full[:16]
    for h in range(1, 8):
        last = jnp.where(head == h, full[16 * h : 16 * h + 16], last)
    return jnp.concatenate([jnp.concatenate(blocks, axis=0).T, last], axis=0)


def head_sum(value, ones_block):
    return nn(value.astype(BF), ones_block)


def head_sum_fine(value, ones_block):
    high = value.astype(BF)
    low = (value - high.astype(F32)).astype(BF)
    return nn(high, ones_block) + nn(low, ones_block)


def pair_math(x, hand_over, split, w_qkv, w_out, w_out_t, gain, scale_cols, scale_lanes, ones_big, minus_ones_t, ones_blk):
    ones_block = ones_blk[...]
    ones4, ones_last = ones_big[0:512, 0:128], ones_big[1024:, :]
    minus4, minus_last = minus_ones_t[0:128, 0:512], minus_ones_t[:, 1024:]
    qkv = nn(x, w_qkv[...]).astype(BF)
    row = lax.broadcasted_iota(jnp.int32, (TOK, 1), 0)
    col = key_token(lax.broadcasted_iota(jnp.int32, (1, KEYS), 1))
    allowed = jnp.where(split, (row // QUART) % 2, 0) == jnp.where(split, (col // QUART) % 2, 0)
    vec = []
    for half in range(2):
        lo = half * 256
        q = qkv[:, lo : lo + 256].astype(F32)
        k = qkv[:, 512 + lo : 768 + lo].astype(F32)
        q_len = jnp.sqrt(head_sum_fine(q * q, ones_block))
        k_len = jnp.sqrt(head_sum_fine(k * k, ones_block))
        q_inv = 1.0 / jnp.maximum(q_len, FLOOR)
        k_inv = 1.0 / jnp.maximum(k_len, FLOOR)
        uq = q * q_inv
        uk = k * k_inv
        vec.append((q_len, k_len, q_inv, k_inv, uq, uk, uq.astype(BF), uk.astype(BF)))
    att = [[None, None], [None, None]]
    saved = {}
    for g in range(2):
        r = slice(g * TOK, (g + 1) * TOK)
        for half in range(2):
            lo = half * 256
            uq, uk = vec[half][6][r], vec[half][7][r]
            v = qkv[r, 1024 + lo : 1280 + lo]
            k_t = uk[:128].T
            scores = [nn(uq[:, 128 * p : 128 * p + 128], cols4(k_t, p)) for p in range(2)]
            scores.append(nn(uq, rows_last(uk).T))
            e = jnp.exp2(jnp.concatenate(scores, axis=1) * scale_cols[half : half + 1, :])
            if g == 1:
                e = jnp.where(allowed, e, 0.0)
            e = e.astype(BF)
            v_last = rows_last(v)
            last = nn(e[:, 1024:], jnp.concatenate([v_last, ones_last], axis=1))
            main = [
                nn(e[:, 512 * p : 512 * p + 512], jnp.concatenate([rows4(v, p), ones4], axis=1)) for p in range(2)
            ]
            num = jnp.concatenate([one[:, :128] for one in main], axis=1) + last[:, :256]
            r_den = 1.0 / (jnp.concatenate([one[:, 128:] for one in main], axis=1) + last[:, 256:])
            att[g][half] = (num * r_den).astype(BF)
            saved[g, half] = (v, v_last, e, r_den, uq, uk)
    att_b = jnp.concatenate([jnp.concatenate(one, axis=1) for one in att], axis=0)
    proj = nn(att_b, w_out[...])
    dev = proj - jnp.mean(proj, -1, keepdims=True)
    inv = lax.rsqrt(jnp.mean(dev * dev, -1, keepdims=True) + EPS)
    normed = dev * inv
    branch = gain * normed
    up = gain * hand_over(branch)
    dproj = (
        (up - jnp.mean(up, -1, keepdims=True) - normed * jnp.mean(up * normed, -1, keepdims=True))
        * inv
    ).astype(BF)
    datt = nn(dproj, w_out_t[...]).astype(BF)
    dq, dk, dv = {}, {}, {}
    for g in range(2):
        r = slice(g * TOK, (g + 1) * TOK)
        for half in range(2):
            lo = half * 256
            v, v_last, e, r_den, uq, uk = saved[g, half]
            dh = datt[r, lo : lo + 256].astype(F32) * r_den
            dh_b = dh.astype(BF)
            dd = (dh * att[g][half].astype(F32)).astype(BF)
            v_t = v[:128].T
            t = []
            for p in range(2):
                lanes = slice(128 * p, 128 * p + 128)
                t.append(
                    nn(
                        jnp.concatenate([dh_b[:, lanes], dd[:, lanes]], axis=1),
                        jnp.concatenate([cols4(v_t, p), minus4], axis=0),
                    )
                )
            t.append(
                nn(jnp.concatenate([dh_b, dd], axis=1), jnp.concatenate([v_last.T, minus_last], axis=0))
            )
            t = jnp.concatenate(t, axis=1)
            ds = (e.astype(F32) * t).astype(BF)
            lanes = scale_lanes[half : half + 1, :]
            duq = [nn(ds[:, 512 * p : 512 * p + 512], rows4(uk, p)) for p in range(2)]
            dq[g, half] = (jnp.concatenate(duq, axis=1) + nn(ds[:, 1024:], rows_last(uk))) * lanes
            dk[g, half] = by_keys(ds, uq) * lanes
            dv[g, half] = by_keys(e, dh_b).astype(BF)
    cols = [None] * 6
    for half in range(2):
        q_len, k_len, q_inv, k_inv, uq, uk, _, _ = vec[half]
        duq = jnp.concatenate([dq[0, half], dq[1, half]], axis=0)
        duk = jnp.concatenate([dk[0, half], dk[1, half]], axis=0)
        q_tail = jnp.where(q_len > FLOOR, uq * head_sum(uq * duq, ones_block), 0.0)
        k_tail = jnp.where(k_len > FLOOR, uk * head_sum(uk * duk, ones_block), 0.0)
        cols[half] = ((duq - q_tail) * q_inv).astype(BF)
        cols[2 + half] = ((duk - k_tail) * k_inv).astype(BF)
        cols[4 + half] = jnp.concatenate([dv[0, half], dv[1, half]], axis=0)
    dqkv = jnp.concatenate(cols, axis=1)
    return att_b, dproj, dqkv


def pack(ref, first_row, rows, first_col):
    low = first_row // 16 * 16
    high = (first_row + rows + 15) // 16 * 16
    parts = []
    for lev in range(2):
        for c in range(first_col, first_col + 6):
            strip = ref[lev, c, low:high, :].astype(F32)
            parts.append(strip[first_row - low : first_row - low + rows])
    return jnp.concatenate(parts, axis=0)


def padded(part):
    return jnp.concatenate([part, jnp.zeros((8, WIDTH), F32)], axis=0).astype(BF)


def piece_of(x_part, g_part):
    pad = jnp.zeros((4, WIDTH), F32)
    return jnp.concatenate([x_part, pad, g_part, pad], axis=0).astype(BF)


def unpiece(ref):
    whole = ref.astype(F32)
    return whole[:QUART], whole[40 : 40 + QUART]


def block_kernel(
    x_hbm,
    g_hbm,
    w_qkv_hbm,
    w_out_hbm,
    gain_ref,
    scale_ref,
    out_hbm,
    gin_hbm,
    gq_ref,
    go_ref,
    x_ref,
    g_ref,
    w_qkv,
    w_out,
    out_ref,
    gin_ref,
    send,
    recv,
    own,
    back_send,
    back_recv,
    own_res,
    send7,
    recv7,
    back7_send,
    back7_recv,
    x_all,
    att_all,
    dproj_all,
    dqkv_all,
    w_qkv_t,
    w_out_t,
    ones_big,
    minus_ones_t,
    ones_blk,
    scale_cols,
    scale_lanes,
    grads,
    pair_recv,
    mine,
    ring_relay,
    ring_recv,
    cut,
    line_recv,
    piece,
    z_recv,
    part,
    whole,
    send_sem,
    recv_sem,
    back_send_sem,
    back_recv_sem,
    send7_sem,
    recv7_sem,
    back7_send_sem,
    back7_recv_sem,
    pair_send_sem,
    pair_recv_sem,
    relay_send_sem,
    relay_recv_sem,
    ring_send_sem,
    ring_recv_sem,
    line_send_sem,
    line_recv_sem,
    z_send_sem,
    z_recv_sem,
    gather_send_sem,
    gather_recv_sem,
    load_sem,
    store_sem,
):
    loads = [
        pltpu.make_async_copy(src, dst, load_sem.at[i])
        for i, (src, dst) in enumerate(((x_hbm, x_ref), (g_hbm, g_ref), (w_qkv_hbm, w_qkv), (w_out_hbm, w_out)))
    ]
    for c in loads:
        c.start()
    n_lat = lax.axis_size("lat")
    n_lon = lax.axis_size("lon")
    a = lax.axis_index("lat")
    b = lax.axis_index("lon")

    def mod(value, n):
        return lax.rem(value + n, n)

    up_a, dn_a = mod(a + 1, n_lat), mod(a - 1, n_lat)
    up_b, dn_b = mod(b + 1, n_lon), mod(b - 1, n_lon)
    core, y_lo = lax.rem(a, 2), a // 2
    z, y_hi, x = b // 8, lax.rem(b // 4, 2), lax.rem(b, 4)
    y = 2 * y_hi + y_lo
    u = x * (1 - core) + y * core
    v = y * (1 - core) + x * core

    def device(uu, vv, zz):
        xx = uu * (1 - core) + vv * core
        yy = vv * (1 - core) + uu * core
        return (2 * lax.rem(yy, 2) + core, zz * 8 + (yy // 2) * 4 + xx)

    partner = (a + 1 - 2 * core, b)
    nxt = device(mod(u + 1, 4), v, z)
    prv = device(mod(u + 3, 4), v, z)
    line = [device(u, mod(v + i, 4), z) for i in range(1, 4)]
    column = [device(u, v, mod(z + i, 8)) for i in range(1, 8)]
    group = [(mod(a + i, 4), b) for i in range(1, 4)]
    around = [(a, up_b), (a, dn_b), (up_a, b), (dn_a, b), (up_a, dn_b), (dn_a, up_b)]
    peers = around + [partner, nxt, prv] + line + column + group

    barrier = pltpu.get_barrier_semaphore()
    for peer in peers:
        pl.semaphore_signal(barrier, inc=1, device_id=peer, device_id_type=MESH)

    def copy(src, dst, send_sem, recv_sem, peer):
        return pltpu.make_async_remote_copy(
            src_ref=src, dst_ref=dst, send_sem=send_sem, recv_sem=recv_sem, device_id=peer, device_id_type=MESH
        )

    def forth(w, k, peer):
        return copy(send.at[w, k], recv.at[w, k], send_sem.at[w, k], recv_sem.at[w, k], peer)

    def back(w, k, peer):
        return copy(back_send.at[w, k], back_recv.at[w, k], back_send_sem.at[w, k], back_recv_sem.at[w, k], peer)

    def forth7(j):
        peer = ((a, up_b), (dn_a, b), (dn_a, up_b))[j]
        return copy(send7.at[j], recv7.at[j], send7_sem.at[j], recv7_sem.at[j], peer)

    def back7(j, k):
        peer = ((a, dn_b), (up_a, b), (up_a, dn_b))[j]
        return copy(
            back7_send.at[j, k], back7_recv.at[j, k], back7_send_sem.at[j, k], back7_recv_sem.at[j, k], peer
        )

    loads[0].wait()
    for w in range(2):
        send[w, 0] = padded(pack(x_ref, 6 * w + 3, 6, 6 * (w % 2)))
    loads[1].wait()
    for w in range(2):
        send[w, 1] = padded(pack(g_ref, 6 * w + 3, 6, 6 * (w % 2)))
    pl.semaphore_wait(barrier, len(peers))
    for k in range(2):
        for w in range(2):
            forth(w, k, (a, up_b) if w % 2 else (a, dn_b)).start()
    for w in range(2, 7):
        for k, ref in enumerate((x_ref, g_ref)):
            send[w, k] = padded(pack(ref, 6 * w + 3, 6, 6 * (w % 2)))
            forth(w, k, (a, up_b) if w % 2 else (a, dn_b)).start()
    for j, (first_row, first_col) in enumerate(((45, 6), (0, 0), (0, 6))):
        send7[j] = piece_of(pack(x_ref, first_row, 3, first_col), pack(g_ref, first_row, 3, first_col))
        forth7(j).start()

    for w in range(7):
        for k, ref in enumerate((x_ref, g_ref)):
            own[w, k] = padded(pack(ref, 6 * w + 3, 6, 6 - 6 * (w % 2)))

    loads[2].wait()
    loads[3].wait()
    w_qkv_t[...] = w_qkv[...].T
    w_out_t[...] = w_out[...].T
    head = lax.broadcasted_iota(jnp.int32, (KEYS, 256), 1) // 32
    place = key_head(lax.broadcasted_iota(jnp.int32, (KEYS, 256), 0))
    ones_big[...] = jnp.where(place == head, 1.0, 0.0).astype(BF)
    head = lax.broadcasted_iota(jnp.int32, (256, KEYS), 0) // 32
    place = key_head(lax.broadcasted_iota(jnp.int32, (256, KEYS), 1))
    minus_ones_t[...] = jnp.where(place == head, -1.0, 0.0).astype(BF)
    head = lax.broadcasted_iota(jnp.int32, (256, 256), 1) // 32
    ones_blk[...] = jnp.where(lax.broadcasted_iota(jnp.int32, (256, 256), 0) // 32 == head, 1.0, 0.0).astype(BF)
    for half in range(2):
        col_head = key_head(lax.broadcasted_iota(jnp.int32, (1, KEYS), 1))
        lane_head = lax.broadcasted_iota(jnp.int32, (1, 256), 1) // 32
        keys = jnp.zeros((1, KEYS), F32)
        lanes = jnp.zeros((1, 256), F32)
        for h in range(8):
            keys = jnp.where(col_head == h, scale_ref[half * 8 + h] * LOG2E, keys)
            lanes = jnp.where(lane_head == h, scale_ref[half * 8 + h], lanes)
        scale_cols[half : half + 1, :] = keys
        scale_lanes[half : half + 1, :] = lanes

    def results(w, part, k, values):
        at = part * TOK
        own_res[w, k, 0:HALF] = values[at : at + HALF].astype(BF)
        back_send[w, k, 0:HALF] = values[at + HALF : at + TOK].astype(BF)

    def send_back7(k):
        ours = own_res[7, k].astype(F32)
        theirs = back_send[7, k].astype(F32)
        pad = jnp.zeros((48 - QUART, WIDTH), F32)
        for j, quarter in enumerate((theirs[:QUART], ours[QUART:HALF], theirs[QUART:HALF])):
            back7_send[j, k] = jnp.concatenate([quarter, pad], axis=0).astype(BF)
            back7(j, k).start()

    for w in range(8):
        for k in range(2):
            back_send[w, k, HALF:] = jnp.zeros((8, WIDTH), BF)

    @pl.loop(0, 4)
    def _(pair):
        w = 2 * pair
        forth(w, 0, (a, up_b)).wait_recv()

        @pl.when(pair < 3)
        def _():
            forth(w + 1, 0, (a, up_b)).wait_recv()

        @pl.when(pair == 3)
        def _():
            for j in range(3):
                forth7(j).wait_recv()
            low = pack(x_ref, 45, 3, 0), pack(g_ref, 45, 3, 0)
            side, down, diag = (unpiece(recv7[j]) for j in range(3))
            for k in range(2):
                own[7, k] = padded(jnp.concatenate([low[k], down[k]], axis=0))
                recv[7, k] = padded(jnp.concatenate([side[k], diag[k]], axis=0))

        def tokens(k):
            blocks = [ref[w + i, k].astype(F32)[:HALF] for i in range(2) for ref in (own, recv)]
            return jnp.concatenate(blocks, axis=0)

        def hand_over(branch):
            for i in range(2):
                results(w + i, i, 0, branch)
            back(w, 0, (a, up_b)).start()
            forth(w, 1, (a, up_b)).wait_recv()

            @pl.when(pair < 3)
            def _():
                back(w + 1, 0, (a, dn_b)).start()
                forth(w + 1, 1, (a, up_b)).wait_recv()

            @pl.when(pair == 3)
            def _():
                send_back7(0)

            return tokens(1)

        xw = tokens(0).astype(BF)
        split = jnp.logical_and(pair == 3, a == n_lat - 1)
        att, dproj, dqkv = pair_math(
            xw,
            hand_over,
            split,
            w_qkv,
            w_out,
            w_out_t,
            gain_ref[...],
            scale_cols,
            scale_lanes,
            ones_big,
            minus_ones_t,
            ones_blk,
        )
        rows = pl.ds(pl.multiple_of(pair * 2 * TOK, 2 * TOK), 2 * TOK)
        x_all[rows, :] = xw
        att_all[rows, :] = att
        dproj_all[rows, :] = dproj
        dqkv_all[rows, :] = dqkv

        dshifted = nn(dqkv, w_qkv_t[...])
        for i in range(2):
            results(w + i, i, 1, dshifted)
        back(w, 1, (a, up_b)).start()

        @pl.when(pair < 3)
        def _():
            back(w + 1, 1, (a, dn_b)).start()

    send_back7(1)

    def columns_of(owner, side):
        at = pl.multiple_of(owner * 768, 256)
        wide = tn(x_all[...], dqkv_all[:, pl.ds(at, 768)])
        chunks = [wide[:, i * 256 : (i + 1) * 256] for i in range(3)]
        chunks.append(tn(dproj_all[...], att_all[:, pl.ds(pl.multiple_of(owner * 256, 256), 256)]))
        for low in range(2):
            halves = [chunk.reshape(64, 8, 256) for chunk in chunks[2 * low : 2 * low + 2]]
            joined = jnp.concatenate(halves, axis=1).astype(BF)
            for lon in range(64):
                zz, yy, xx = lon // 8, 2 * ((lon // 4) % 2) + low, lon % 4
                uu = xx * (1 - owner) + yy * owner
                vv = yy * (1 - owner) + xx * owner
                grads[side, uu, vv, zz] = joined[lon]

    columns_of(1 - core, 0)

    order = (2, 1, 3, 0)
    pairs = []
    for i, step in enumerate(order):
        c = copy(grads.at[0, mod(v + step, 4)], pair_recv.at[i], pair_send_sem.at[i], pair_recv_sem.at[i], partner)
        c.start()
        pairs.append(c)

    columns_of(core, 1)

    def add_pair(i):
        pairs[i].wait_recv()
        chunk = mod(u + order[i], 4)

        @pl.loop(0, 4)
        def _(vv):
            mine[i, vv] = (grads[1, chunk, vv].astype(F32) + pair_recv[i, vv].astype(F32)).astype(BF)

    def assemble(k, lev, left):
        parts = []
        for w in range(7):
            came = (w % 2 == 0) == left
            parts.append((back_recv if came else own_res)[w, k].astype(F32))
        top = back7_recv[1 if left else 2, k].astype(F32)
        low = (own_res[7, k] if left else back7_recv[0, k]).astype(F32)
        ref, dst, hbm = ((x_ref, out_ref, out_hbm), (g_ref, gin_ref, gin_hbm))[k]
        for c in range(6):
            at = lev * 6 + c
            strip = (
                [top[at * 3 : at * 3 + 3]] + [one[at * 6 : at * 6 + 6] for one in parts] + [low[at * 3 : at * 3 + 3]]
            )
            cc = c if left else c + 6
            dst[lev, cc] = (ref[lev, cc].astype(F32) + jnp.concatenate(strip, axis=0)).astype(BF)
        place = pl.ds(0 if left else 6, 6)
        i = (2 * lev + (0 if left else 1)) * 2 + k
        c = pltpu.make_async_copy(dst.at[lev, place], hbm.at[lev, place], store_sem.at[i])
        c.start()
        stores.append(c)

    def wait_back(k):
        for w in range(7):
            back(w, k, (a, up_b)).wait_recv()
        for j in range(3):
            back7(j, k).wait_recv()

    stores = []

    add_pair(0)
    relay_up = copy(mine.at[0, pl.ds(0, 2)], ring_relay.at[0], relay_send_sem.at[0], relay_recv_sem.at[0], nxt)
    relay_dn = copy(mine.at[0, pl.ds(2, 2)], ring_relay.at[1], relay_send_sem.at[1], relay_recv_sem.at[1], prv)
    relay_up.start()
    relay_dn.start()
    add_pair(1)
    ring_up_b = copy(mine.at[1, pl.ds(2, 2)], ring_recv.at[0, pl.ds(2, 2)], ring_send_sem.at[0], ring_recv_sem.at[0], nxt)
    ring_up_b.start()
    add_pair(2)
    ring_dn_a = copy(mine.at[2, pl.ds(0, 2)], ring_recv.at[1, pl.ds(0, 2)], ring_send_sem.at[1], ring_recv_sem.at[1], prv)
    ring_dn_a.start()
    add_pair(3)
    relay_up.wait_recv()

    @pl.loop(0, 2)
    def _(vv):
        mine[1, vv] = (mine[1, vv].astype(F32) + ring_relay[0, vv].astype(F32)).astype(BF)

    ring_up_a = copy(mine.at[1, pl.ds(0, 2)], ring_recv.at[0, pl.ds(0, 2)], ring_send_sem.at[2], ring_recv_sem.at[2], nxt)
    ring_up_a.start()
    relay_dn.wait_recv()

    @pl.loop(0, 2)
    def _(vv):
        mine[2, 2 + vv] = (mine[2, 2 + vv].astype(F32) + ring_relay[1, vv].astype(F32)).astype(BF)

    ring_dn_b = copy(mine.at[2, pl.ds(2, 2)], ring_recv.at[1, pl.ds(2, 2)], ring_send_sem.at[3], ring_recv_sem.at[3], prv)
    ring_dn_b.start()

    wait_back(0)
    assemble(0, 0, True)
    assemble(0, 0, False)

    for c in (ring_up_b, ring_dn_a, ring_up_a, ring_dn_b):
        c.wait_recv()

    @pl.loop(0, 4)
    def _(vv):
        cut[vv] = (
            mine[3, vv].astype(F32) + ring_recv[0, vv].astype(F32) + ring_recv[1, vv].astype(F32)
        ).astype(BF)

    lines = []
    for i in range(3):
        c = copy(cut.at[mod(v + i + 1, 4)], line_recv.at[i], line_send_sem.at[i], line_recv_sem.at[i], line[i])
        c.start()
        lines.append(c)
    assemble(0, 1, True)
    for c in lines:
        c.wait_recv()
    piece[...] = (
        cut[v].astype(F32) + line_recv[0].astype(F32) + line_recv[1].astype(F32) + line_recv[2].astype(F32)
    ).astype(BF)
    columns = []
    for i in range(7):
        c = copy(piece.at[mod(z + i + 1, 8)], z_recv.at[i], z_send_sem.at[i], z_recv_sem.at[i], column[i])
        c.start()
        columns.append(c)
    assemble(0, 1, False)
    for c in columns:
        c.wait_recv()
    total = piece[z].astype(F32)
    for i in range(7):
        total = total + z_recv[i].astype(F32)
    part[...] = total

    here = 2 * core + y_lo
    whole[here] = total
    gathers = []
    for i in range(3):
        c = copy(part, whole.at[here], gather_send_sem.at[i], gather_recv_sem.at[i], group[i])
        c.start()
        gathers.append(c)

    wait_back(1)
    for lev in range(2):
        for left in (True, False):
            assemble(1, lev, left)

    for w in range(7):
        for k in range(2):
            forth(w, k, (a, up_b)).wait_send()
            back(w, k, (a, up_b)).wait_send()
    for j in range(3):
        forth7(j).wait_send()
        for k in range(2):
            back7(j, k).wait_send()
    for c in pairs + [relay_up, relay_dn, ring_up_b, ring_dn_a, ring_up_a, ring_dn_b] + lines + columns:
        c.wait_send()
    for c in gathers:
        c.wait_recv()
    for owner in range(2):
        at = owner * 768
        gq_ref[:, at : at + 256] = whole[2 * owner, 0:8, :]
        gq_ref[:, at + 256 : at + 512] = whole[2 * owner, 8:16, :]
        gq_ref[:, at + 512 : at + 768] = whole[2 * owner + 1, 0:8, :]
        go_ref[:, owner * 256 : owner * 256 + 256] = whole[2 * owner + 1, 8:16, :]
    for c in gathers:
        c.wait_send()
    for c in stores:
        c.wait()


def move_kernel(*refs):
    sources, targets, held, in_sem, out_sem = refs[:4], refs[4:8], refs[8:12], refs[12], refs[13]
    moves = []
    for i in range(4):
        for part in range(2) if i < 2 else (0,):
            n = len(moves)
            views = [ref.at[part] if i < 2 else ref for ref in (sources[i], held[i], targets[i])]
            first = pltpu.make_async_copy(views[0], views[1], in_sem.at[n])
            second = pltpu.make_async_copy(views[1], views[2], out_sem.at[n])
            first.start()
            moves.append((first, second))
    for first, second in moves:
        first.wait()
        second.start()
    for first, second in moves:
        second.wait()


def body(inputs, cotangent, w_qkv, w_out, gain, logit_scale):
    vmem = pl.BlockSpec(memory_space=pltpu.VMEM)
    smem = pl.BlockSpec(memory_space=pltpu.SMEM)
    dma = pltpu.SemaphoreType.DMA
    anywhere = pl.BlockSpec(memory_space=pl.ANY)
    halves = pltpu.VMEM((8, 2, 80, WIDTH), BF)
    pieces = pltpu.VMEM((3, 80, WIDTH), BF)
    quarters = pltpu.VMEM((3, 2, 48, WIDTH), BF)
    x_view = inputs.transpose(0, 2, 1, 3)
    g_view = cotangent.transpose(0, 2, 1, 3)
    out, grad_in, share_qkv, share_out = pl.pallas_call(
        block_kernel,
        out_shape=[
            jax.ShapeDtypeStruct(x_view.shape, BF),
            jax.ShapeDtypeStruct(x_view.shape, BF),
            jax.ShapeDtypeStruct((8, 3 * WIDTH), F32),
            jax.ShapeDtypeStruct((8, WIDTH), F32),
        ],
        in_specs=[anywhere] * 4 + [vmem, smem],
        out_specs=[anywhere] * 2 + [vmem] * 2,
        scratch_shapes=[
            pltpu.VMEM(x_view.shape, BF),
            pltpu.VMEM(x_view.shape, BF),
            pltpu.VMEM(w_qkv.shape, BF),
            pltpu.VMEM(w_out.shape, BF),
            pltpu.VMEM(x_view.shape, BF),
            pltpu.VMEM(x_view.shape, BF),
        ]
        + [halves] * 6
        + [pieces] * 2
        + [quarters] * 2
        + [
            pltpu.VMEM((8 * TOK, WIDTH), BF),
            pltpu.VMEM((8 * TOK, WIDTH), BF),
            pltpu.VMEM((8 * TOK, WIDTH), BF),
            pltpu.VMEM((8 * TOK, 3 * WIDTH), BF),
            pltpu.VMEM((3 * WIDTH, WIDTH), BF),
            pltpu.VMEM((WIDTH, WIDTH), BF),
            pltpu.VMEM((KEYS, 256), BF),
            pltpu.VMEM((256, KEYS), BF),
            pltpu.VMEM((256, 256), BF),
            pltpu.VMEM((2, KEYS), F32),
            pltpu.VMEM((2, 256), F32),
            pltpu.VMEM((2, 4, 4, 8, 16, 256), BF),
            pltpu.VMEM((4, 4, 8, 16, 256), BF),
            pltpu.VMEM((4, 4, 8, 16, 256), BF),
            pltpu.VMEM((2, 2, 8, 16, 256), BF),
            pltpu.VMEM((2, 4, 8, 16, 256), BF),
            pltpu.VMEM((4, 8, 16, 256), BF),
            pltpu.VMEM((3, 8, 16, 256), BF),
            pltpu.VMEM((8, 16, 256), BF),
            pltpu.VMEM((7, 16, 256), BF),
            pltpu.VMEM((16, 256), F32),
            pltpu.VMEM((4, 16, 256), F32),
        ]
        + [dma((7, 2))] * 4
        + [dma((3,))] * 2
        + [dma((3, 2))] * 2
        + [dma((4,))] * 2
        + [dma((2,))] * 2
        + [dma((4,))] * 2
        + [dma((3,))] * 2
        + [dma((7,))] * 2
        + [dma((3,))] * 2
        + [dma((4,)), dma((8,))],
        compiler_params=pltpu.CompilerParams(
            collective_id=0, has_side_effects=True, vmem_limit_bytes=56 * 2**20
        ),
    )(x_view, g_view, w_qkv, w_out, gain.reshape(1, WIDTH), logit_scale)
    results = (out, grad_in, share_qkv, share_out)
    out, grad_in, share_qkv, share_out = pl.pallas_call(
        move_kernel,
        out_shape=[jax.ShapeDtypeStruct(r.shape, r.dtype) for r in results],
        in_specs=[anywhere] * 4,
        out_specs=[anywhere] * 4,
        scratch_shapes=[pltpu.VMEM(r.shape, r.dtype) for r in results] + [dma((6,)), dma((6,))],
    )(*results)
    return out.transpose(0, 2, 1, 3), grad_in.transpose(0, 2, 1, 3), share_qkv, share_out.T


def solution(mesh):
    placed = (P(None, "lat", "lon", None), P(None, "lat", "lon", None), P(), P(), P(), P())
    return jax.shard_map(
        body,
        mesh=mesh,
        in_specs=placed,
        out_specs=(
            P(None, "lat", "lon", None),
            P(None, "lat", "lon", None),
            P("lon", None),
            P(None, "lon"),
        ),
        check_vma=False,
    )
```

```python
import jax
import jax.numpy as jnp
from jax import lax
from jax.experimental import pallas as pl
from jax.experimental.pallas import tpu as pltpu
from jax.sharding import PartitionSpec as P

BF = jnp.bfloat16
F32 = jnp.float32
MESH = pl.DeviceIdType.MESH
HEADS = 16
WIDTH = 512
HALF = 72
TOK = 144
QUART = 36
KEYS = 8 * TOK
LOG2E = 1.4426950408889634
FLOOR = 1e-6
EPS = 1e-5


def nn(a, b):
    return jnp.dot(a, b, preferred_element_type=F32)


def nt(a, b):
    return lax.dot_general(a, b, (((1,), (1,)), ((), ())), preferred_element_type=F32)


def tn(a, b):
    return lax.dot_general(a, b, (((0,), (0,)), ((), ())), preferred_element_type=F32)


def key_head(place):
    return jnp.where(place < 1024, place // 128, (place - 1024) // 16)


def key_token(place):
    return jnp.where(place < 1024, place % 128, 128 + (place - 1024) % 16)


def alone(part, axis, heads):
    head = lax.broadcasted_iota(jnp.int32, part.shape, axis) // 32
    zero = jnp.zeros_like(part)
    return [jnp.where(head == h, part, zero) for h in range(heads)]


def rows4(part, p):
    return jnp.concatenate(alone(part[:128, 128 * p : 128 * p + 128], 1, 4), axis=0)


def rows_last(part):
    return jnp.concatenate(alone(part[128:], 1, 8), axis=0)


def cols4(main_t, p):
    return jnp.concatenate(alone(main_t[128 * p : 128 * p + 128], 0, 4), axis=1)


def by_keys(e, d):
    d_t = d.T
    blocks = []
    for p in range(4):
        two = nn(d_t[64 * p : 64 * p + 64], e[:, 256 * p : 256 * p + 256])
        blocks += [two[:32, :128], two[32:, 128:]]
    full = tn(e[:, 1024:], d)
    head = lax.broadcasted_iota(jnp.int32, (16, 256), 1) // 32
    last = full[:16]
    for h in range(1, 8):
        last = jnp.where(head == h, full[16 * h : 16 * h + 16], last)
    return jnp.concatenate([jnp.concatenate(blocks, axis=0).T, last], axis=0)


def head_sum(value, ones_block):
    return nn(value.astype(BF), ones_block)


def head_sum_fine(value, ones_block):
    high = value.astype(BF)
    low = (value - high.astype(F32)).astype(BF)
    return nn(high, ones_block) + nn(low, ones_block)


def pair_math(x, hand_over, split, w_qkv, w_out, w_out_t, gain, scale_cols, scale_lanes, ones_big, minus_ones_t, ones_blk):
    ones_block = ones_blk[...]
    ones4, ones_last = ones_big[0:512, 0:128], ones_big[1024:, :]
    minus4, minus_last = minus_ones_t[0:128, 0:512], minus_ones_t[:, 1024:]
    qkv = nn(x, w_qkv[...]).astype(BF)
    row = lax.broadcasted_iota(jnp.int32, (TOK, 1), 0)
    col = key_token(lax.broadcasted_iota(jnp.int32, (1, KEYS), 1))
    allowed = jnp.where(split, (row // QUART) % 2, 0) == jnp.where(split, (col // QUART) % 2, 0)
    vec = []
    for half in range(2):
        lo = half * 256
        q = qkv[:, lo : lo + 256].astype(F32)
        k = qkv[:, 512 + lo : 768 + lo].astype(F32)
        q_len = jnp.sqrt(head_sum_fine(q * q, ones_block))
        k_len = jnp.sqrt(head_sum_fine(k * k, ones_block))
        q_inv = 1.0 / jnp.maximum(q_len, FLOOR)
        k_inv = 1.0 / jnp.maximum(k_len, FLOOR)
        uq = q * q_inv
        uk = k * k_inv
        vec.append((q_len, k_len, q_inv, k_inv, uq, uk, uq.astype(BF), uk.astype(BF)))
    att = [[None, None], [None, None]]
    saved = {}
    for g in range(2):
        r = slice(g * TOK, (g + 1) * TOK)
        for half in range(2):
            lo = half * 256
            uq, uk = vec[half][6][r], vec[half][7][r]
            v = qkv[r, 1024 + lo : 1280 + lo]
            k_t = uk[:128].T
            scores = [nn(uq[:, 128 * p : 128 * p + 128], cols4(k_t, p)) for p in range(2)]
            scores.append(nn(uq, rows_last(uk).T))
            e = jnp.exp2(jnp.concatenate(scores, axis=1) * scale_cols[half : half + 1, :])
            if g == 1:
                e = jnp.where(allowed, e, 0.0)
            e = e.astype(BF)
            v_last = rows_last(v)
            last = nn(e[:, 1024:], jnp.concatenate([v_last, ones_last], axis=1))
            main = [
                nn(e[:, 512 * p : 512 * p + 512], jnp.concatenate([rows4(v, p), ones4], axis=1)) for p in range(2)
            ]
            num = jnp.concatenate([one[:, :128] for one in main], axis=1) + last[:, :256]
            r_den = 1.0 / (jnp.concatenate([one[:, 128:] for one in main], axis=1) + last[:, 256:])
            att[g][half] = (num * r_den).astype(BF)
            saved[g, half] = (v, v_last, e, r_den, uq, uk)
    att_b = jnp.concatenate([jnp.concatenate(one, axis=1) for one in att], axis=0)
    proj = nn(att_b, w_out[...])
    dev = proj - jnp.mean(proj, -1, keepdims=True)
    inv = lax.rsqrt(jnp.mean(dev * dev, -1, keepdims=True) + EPS)
    normed = dev * inv
    branch = gain * normed
    up = gain * hand_over(branch)
    dproj = (
        (up - jnp.mean(up, -1, keepdims=True) - normed * jnp.mean(up * normed, -1, keepdims=True))
        * inv
    ).astype(BF)
    datt = nn(dproj, w_out_t[...]).astype(BF)
    dq, dk, dv = {}, {}, {}
    for g in range(2):
        r = slice(g * TOK, (g + 1) * TOK)
        for half in range(2):
            lo = half * 256
            v, v_last, e, r_den, uq, uk = saved[g, half]
            dh = datt[r, lo : lo + 256].astype(F32) * r_den
            dh_b = dh.astype(BF)
            dd = (dh * att[g][half].astype(F32)).astype(BF)
            v_t = v[:128].T
            t = []
            for p in range(2):
                lanes = slice(128 * p, 128 * p + 128)
                t.append(
                    nn(
                        jnp.concatenate([dh_b[:, lanes], dd[:, lanes]], axis=1),
                        jnp.concatenate([cols4(v_t, p), minus4], axis=0),
                    )
                )
            t.append(
                nn(jnp.concatenate([dh_b, dd], axis=1), jnp.concatenate([v_last.T, minus_last], axis=0))
            )
            t = jnp.concatenate(t, axis=1)
            ds = (e.astype(F32) * t).astype(BF)
            lanes = scale_lanes[half : half + 1, :]
            duq = [nn(ds[:, 512 * p : 512 * p + 512], rows4(uk, p)) for p in range(2)]
            dq[g, half] = (jnp.concatenate(duq, axis=1) + nn(ds[:, 1024:], rows_last(uk))) * lanes
            dk[g, half] = by_keys(ds, uq) * lanes
            dv[g, half] = by_keys(e, dh_b).astype(BF)
    cols = [None] * 6
    for half in range(2):
        q_len, k_len, q_inv, k_inv, uq, uk, _, _ = vec[half]
        duq = jnp.concatenate([dq[0, half], dq[1, half]], axis=0)
        duk = jnp.concatenate([dk[0, half], dk[1, half]], axis=0)
        q_tail = jnp.where(q_len > FLOOR, uq * head_sum(uq * duq, ones_block), 0.0)
        k_tail = jnp.where(k_len > FLOOR, uk * head_sum(uk * duk, ones_block), 0.0)
        cols[half] = ((duq - q_tail) * q_inv).astype(BF)
        cols[2 + half] = ((duk - k_tail) * k_inv).astype(BF)
        cols[4 + half] = jnp.concatenate([dv[0, half], dv[1, half]], axis=0)
    dqkv = jnp.concatenate(cols, axis=1)
    return att_b, dproj, dqkv


def pack(ref, first_row, rows, first_col):
    low = first_row // 16 * 16
    high = (first_row + rows + 15) // 16 * 16
    parts = []
    for lev in range(2):
        for c in range(first_col, first_col + 6):
            strip = ref[lev, c, low:high, :].astype(F32)
            parts.append(strip[first_row - low : first_row - low + rows])
    return jnp.concatenate(parts, axis=0)


def padded(part):
    return jnp.concatenate([part, jnp.zeros((8, WIDTH), F32)], axis=0).astype(BF)


def piece_of(x_part, g_part):
    pad = jnp.zeros((4, WIDTH), F32)
    return jnp.concatenate([x_part, pad, g_part, pad], axis=0).astype(BF)


def unpiece(ref):
    whole = ref.astype(F32)
    return whole[:QUART], whole[40 : 40 + QUART]


def block_kernel(
    x_hbm,
    g_hbm,
    w_qkv_hbm,
    w_out_hbm,
    gain_ref,
    scale_ref,
    out_hbm,
    gin_hbm,
    gq_ref,
    go_ref,
    x_ref,
    g_ref,
    w_qkv,
    w_out,
    out_ref,
    gin_ref,
    send,
    recv,
    own,
    back_send,
    back_recv,
    own_res,
    send7,
    recv7,
    back7_send,
    back7_recv,
    x_all,
    att_all,
    dproj_all,
    dqkv_all,
    w_qkv_t,
    w_out_t,
    ones_big,
    minus_ones_t,
    ones_blk,
    scale_cols,
    scale_lanes,
    grads,
    pair_recv,
    mine,
    ring_relay,
    ring_recv,
    cut,
    line_recv,
    piece,
    z_recv,
    part,
    whole,
    send_sem,
    recv_sem,
    back_send_sem,
    back_recv_sem,
    send7_sem,
    recv7_sem,
    back7_send_sem,
    back7_recv_sem,
    pair_send_sem,
    pair_recv_sem,
    relay_send_sem,
    relay_recv_sem,
    ring_send_sem,
    ring_recv_sem,
    line_send_sem,
    line_recv_sem,
    z_send_sem,
    z_recv_sem,
    gather_send_sem,
    gather_recv_sem,
    load_sem,
    store_sem,
):
    loads = [
        pltpu.make_async_copy(src, dst, load_sem.at[i])
        for i, (src, dst) in enumerate(((x_hbm, x_ref), (g_hbm, g_ref), (w_qkv_hbm, w_qkv), (w_out_hbm, w_out)))
    ]
    for c in loads:
        c.start()
    n_lat = lax.axis_size("lat")
    n_lon = lax.axis_size("lon")
    a = lax.axis_index("lat")
    b = lax.axis_index("lon")

    def mod(value, n):
        return lax.rem(value + n, n)

    up_a, dn_a = mod(a + 1, n_lat), mod(a - 1, n_lat)
    up_b, dn_b = mod(b + 1, n_lon), mod(b - 1, n_lon)
    core, y_lo = lax.rem(a, 2), a // 2
    z, y_hi, x = b // 8, lax.rem(b // 4, 2), lax.rem(b, 4)
    y = 2 * y_hi + y_lo
    u = x * (1 - core) + y * core
    v = y * (1 - core) + x * core

    def device(uu, vv, zz):
        xx = uu * (1 - core) + vv * core
        yy = vv * (1 - core) + uu * core
        return (2 * lax.rem(yy, 2) + core, zz * 8 + (yy // 2) * 4 + xx)

    partner = (a + 1 - 2 * core, b)
    nxt = device(mod(u + 1, 4), v, z)
    prv = device(mod(u + 3, 4), v, z)
    line = [device(u, mod(v + i, 4), z) for i in range(1, 4)]
    column = [device(u, v, mod(z + i, 8)) for i in range(1, 8)]
    group = [(mod(a + i, 4), b) for i in range(1, 4)]
    around = [(a, up_b), (a, dn_b), (up_a, b), (dn_a, b), (up_a, dn_b), (dn_a, up_b)]
    peers = around + [partner, nxt, prv] + line + column + group

    barrier = pltpu.get_barrier_semaphore()
    for peer in peers:
        pl.semaphore_signal(barrier, inc=1, device_id=peer, device_id_type=MESH)

    def copy(src, dst, send_sem, recv_sem, peer):
        return pltpu.make_async_remote_copy(
            src_ref=src, dst_ref=dst, send_sem=send_sem, recv_sem=recv_sem, device_id=peer, device_id_type=MESH
        )

    def forth(w, k, peer):
        return copy(send.at[w, k], recv.at[w, k], send_sem.at[w, k], recv_sem.at[w, k], peer)

    def back(w, k, peer):
        return copy(back_send.at[w, k], back_recv.at[w, k], back_send_sem.at[w, k], back_recv_sem.at[w, k], peer)

    def forth7(j):
        peer = ((a, up_b), (dn_a, b), (dn_a, up_b))[j]
        return copy(send7.at[j], recv7.at[j], send7_sem.at[j], recv7_sem.at[j], peer)

    def back7(j, k):
        peer = ((a, dn_b), (up_a, b), (up_a, dn_b))[j]
        return copy(
            back7_send.at[j, k], back7_recv.at[j, k], back7_send_sem.at[j, k], back7_recv_sem.at[j, k], peer
        )

    loads[0].wait()
    for w in range(2):
        send[w, 0] = padded(pack(x_ref, 6 * w + 3, 6, 6 * (w % 2)))
    loads[1].wait()
    for w in range(2):
        send[w, 1] = padded(pack(g_ref, 6 * w + 3, 6, 6 * (w % 2)))
    pl.semaphore_wait(barrier, len(peers))
    for k in range(2):
        for w in range(2):
            forth(w, k, (a, up_b) if w % 2 else (a, dn_b)).start()
    for w in range(2, 7):
        for k, ref in enumerate((x_ref, g_ref)):
            send[w, k] = padded(pack(ref, 6 * w + 3, 6, 6 * (w % 2)))
            forth(w, k, (a, up_b) if w % 2 else (a, dn_b)).start()
    for j, (first_row, first_col) in enumerate(((45, 6), (0, 0), (0, 6))):
        send7[j] = piece_of(pack(x_ref, first_row, 3, first_col), pack(g_ref, first_row, 3, first_col))
        forth7(j).start()

    for w in range(7):
        for k, ref in enumerate((x_ref, g_ref)):
            own[w, k] = padded(pack(ref, 6 * w + 3, 6, 6 - 6 * (w % 2)))

    loads[2].wait()
    loads[3].wait()
    w_qkv_t[...] = w_qkv[...].T
    w_out_t[...] = w_out[...].T
    head = lax.broadcasted_iota(jnp.int32, (KEYS, 256), 1) // 32
    place = key_head(lax.broadcasted_iota(jnp.int32, (KEYS, 256), 0))
    ones_big[...] = jnp.where(place == head, 1.0, 0.0).astype(BF)
    head = lax.broadcasted_iota(jnp.int32, (256, KEYS), 0) // 32
    place = key_head(lax.broadcasted_iota(jnp.int32, (256, KEYS), 1))
    minus_ones_t[...] = jnp.where(place == head, -1.0, 0.0).astype(BF)
    head = lax.broadcasted_iota(jnp.int32, (256, 256), 1) // 32
    ones_blk[...] = jnp.where(lax.broadcasted_iota(jnp.int32, (256, 256), 0) // 32 == head, 1.0, 0.0).astype(BF)
    for half in range(2):
        col_head = key_head(lax.broadcasted_iota(jnp.int32, (1, KEYS), 1))
        lane_head = lax.broadcasted_iota(jnp.int32, (1, 256), 1) // 32
        keys = jnp.zeros((1, KEYS), F32)
        lanes = jnp.zeros((1, 256), F32)
        for h in range(8):
            keys = jnp.where(col_head == h, scale_ref[half * 8 + h] * LOG2E, keys)
            lanes = jnp.where(lane_head == h, scale_ref[half * 8 + h], lanes)
        scale_cols[half : half + 1, :] = keys
        scale_lanes[half : half + 1, :] = lanes

    def results(w, part, k, values):
        at = part * TOK
        own_res[w, k] = padded(values[at : at + HALF])
        back_send[w, k] = padded(values[at + HALF : at + TOK])

    def send_back7(k):
        ours = own_res[7, k].astype(F32)
        theirs = back_send[7, k].astype(F32)
        pad = jnp.zeros((48 - QUART, WIDTH), F32)
        for j, quarter in enumerate((theirs[:QUART], ours[QUART:HALF], theirs[QUART:HALF])):
            back7_send[j, k] = jnp.concatenate([quarter, pad], axis=0).astype(BF)
            back7(j, k).start()

    @pl.loop(0, 4)
    def _(pair):
        w = 2 * pair
        forth(w, 0, (a, up_b)).wait_recv()

        @pl.when(pair < 3)
        def _():
            forth(w + 1, 0, (a, up_b)).wait_recv()

        @pl.when(pair == 3)
        def _():
            for j in range(3):
                forth7(j).wait_recv()
            low = pack(x_ref, 45, 3, 0), pack(g_ref, 45, 3, 0)
            side, down, diag = (unpiece(recv7[j]) for j in range(3))
            for k in range(2):
                own[7, k] = padded(jnp.concatenate([low[k], down[k]], axis=0))
                recv[7, k] = padded(jnp.concatenate([side[k], diag[k]], axis=0))

        def tokens(k):
            blocks = [ref[w + i, k].astype(F32)[:HALF] for i in range(2) for ref in (own, recv)]
            return jnp.concatenate(blocks, axis=0)

        def hand_over(branch):
            for i in range(2):
                results(w + i, i, 0, branch)
            back(w, 0, (a, up_b)).start()
            forth(w, 1, (a, up_b)).wait_recv()

            @pl.when(pair < 3)
            def _():
                back(w + 1, 0, (a, dn_b)).start()
                forth(w + 1, 1, (a, up_b)).wait_recv()

            @pl.when(pair == 3)
            def _():
                send_back7(0)

            return tokens(1)

        xw = tokens(0).astype(BF)
        split = jnp.logical_and(pair == 3, a == n_lat - 1)
        att, dproj, dqkv = pair_math(
            xw,
            hand_over,
            split,
            w_qkv,
            w_out,
            w_out_t,
            gain_ref[...],
            scale_cols,
            scale_lanes,
            ones_big,
            minus_ones_t,
            ones_blk,
        )
        rows = pl.ds(pl.multiple_of(pair * 2 * TOK, 2 * TOK), 2 * TOK)
        x_all[rows, :] = xw
        att_all[rows, :] = att
        dproj_all[rows, :] = dproj
        dqkv_all[rows, :] = dqkv

        dshifted = nn(dqkv, w_qkv_t[...])
        for i in range(2):
            results(w + i, i, 1, dshifted)
        back(w, 1, (a, up_b)).start()

        @pl.when(pair < 3)
        def _():
            back(w + 1, 1, (a, dn_b)).start()

    send_back7(1)

    def columns_of(owner, side):
        at = pl.multiple_of(owner * 768, 256)
        wide = tn(x_all[...], dqkv_all[:, pl.ds(at, 768)])
        chunks = [wide[:, i * 256 : (i + 1) * 256] for i in range(3)]
        chunks.append(tn(dproj_all[...], att_all[:, pl.ds(pl.multiple_of(owner * 256, 256), 256)]))
        for low in range(2):
            halves = [chunk.reshape(64, 8, 256) for chunk in chunks[2 * low : 2 * low + 2]]
            joined = jnp.concatenate(halves, axis=1).astype(BF)
            for lon in range(64):
                zz, yy, xx = lon // 8, 2 * ((lon // 4) % 2) + low, lon % 4
                uu = xx * (1 - owner) + yy * owner
                vv = yy * (1 - owner) + xx * owner
                grads[side, uu, vv, zz] = joined[lon]

    columns_of(1 - core, 0)

    order = (2, 1, 3, 0)
    pairs = []
    for i, step in enumerate(order):
        c = copy(grads.at[0, mod(v + step, 4)], pair_recv.at[i], pair_send_sem.at[i], pair_recv_sem.at[i], partner)
        c.start()
        pairs.append(c)

    columns_of(core, 1)

    def add_pair(i):
        pairs[i].wait_recv()
        chunk = mod(u + order[i], 4)

        @pl.loop(0, 4)
        def _(vv):
            mine[i, vv] = (grads[1, chunk, vv].astype(F32) + pair_recv[i, vv].astype(F32)).astype(BF)

    def assemble(k, lev, left):
        parts = []
        for w in range(7):
            came = (w % 2 == 0) == left
            parts.append((back_recv if came else own_res)[w, k].astype(F32))
        top = back7_recv[1 if left else 2, k].astype(F32)
        low = (own_res[7, k] if left else back7_recv[0, k]).astype(F32)
        ref, dst, hbm = ((x_ref, out_ref, out_hbm), (g_ref, gin_ref, gin_hbm))[k]
        for c in range(6):
            at = lev * 6 + c
            strip = (
                [top[at * 3 : at * 3 + 3]] + [one[at * 6 : at * 6 + 6] for one in parts] + [low[at * 3 : at * 3 + 3]]
            )
            cc = c if left else c + 6
            dst[lev, cc] = (ref[lev, cc].astype(F32) + jnp.concatenate(strip, axis=0)).astype(BF)
        place = pl.ds(0 if left else 6, 6)
        i = (2 * lev + (0 if left else 1)) * 2 + k
        c = pltpu.make_async_copy(dst.at[lev, place], hbm.at[lev, place], store_sem.at[i])
        c.start()
        stores.append(c)

    def wait_back(k):
        for w in range(7):
            back(w, k, (a, up_b)).wait_recv()
        for j in range(3):
            back7(j, k).wait_recv()

    stores = []

    add_pair(0)
    relay_up = copy(mine.at[0, pl.ds(0, 2)], ring_relay.at[0], relay_send_sem.at[0], relay_recv_sem.at[0], nxt)
    relay_dn = copy(mine.at[0, pl.ds(2, 2)], ring_relay.at[1], relay_send_sem.at[1], relay_recv_sem.at[1], prv)
    relay_up.start()
    relay_dn.start()
    add_pair(1)
    ring_up_b = copy(mine.at[1, pl.ds(2, 2)], ring_recv.at[0, pl.ds(2, 2)], ring_send_sem.at[0], ring_recv_sem.at[0], nxt)
    ring_up_b.start()
    add_pair(2)
    ring_dn_a = copy(mine.at[2, pl.ds(0, 2)], ring_recv.at[1, pl.ds(0, 2)], ring_send_sem.at[1], ring_recv_sem.at[1], prv)
    ring_dn_a.start()
    add_pair(3)
    relay_up.wait_recv()

    @pl.loop(0, 2)
    def _(vv):
        mine[1, vv] = (mine[1, vv].astype(F32) + ring_relay[0, vv].astype(F32)).astype(BF)

    ring_up_a = copy(mine.at[1, pl.ds(0, 2)], ring_recv.at[0, pl.ds(0, 2)], ring_send_sem.at[2], ring_recv_sem.at[2], nxt)
    ring_up_a.start()
    relay_dn.wait_recv()

    @pl.loop(0, 2)
    def _(vv):
        mine[2, 2 + vv] = (mine[2, 2 + vv].astype(F32) + ring_relay[1, vv].astype(F32)).astype(BF)

    ring_dn_b = copy(mine.at[2, pl.ds(2, 2)], ring_recv.at[1, pl.ds(2, 2)], ring_send_sem.at[3], ring_recv_sem.at[3], prv)
    ring_dn_b.start()

    wait_back(0)
    assemble(0, 0, True)
    assemble(0, 0, False)

    for c in (ring_up_b, ring_dn_a, ring_up_a, ring_dn_b):
        c.wait_recv()

    @pl.loop(0, 4)
    def _(vv):
        cut[vv] = (
            mine[3, vv].astype(F32) + ring_recv[0, vv].astype(F32) + ring_recv[1, vv].astype(F32)
        ).astype(BF)

    lines = []
    for i in range(3):
        c = copy(cut.at[mod(v + i + 1, 4)], line_recv.at[i], line_send_sem.at[i], line_recv_sem.at[i], line[i])
        c.start()
        lines.append(c)
    assemble(0, 1, True)
    for c in lines:
        c.wait_recv()
    piece[...] = (
        cut[v].astype(F32) + line_recv[0].astype(F32) + line_recv[1].astype(F32) + line_recv[2].astype(F32)
    ).astype(BF)
    columns = []
    for i in range(7):
        c = copy(piece.at[mod(z + i + 1, 8)], z_recv.at[i], z_send_sem.at[i], z_recv_sem.at[i], column[i])
        c.start()
        columns.append(c)
    assemble(0, 1, False)
    for c in columns:
        c.wait_recv()
    total = piece[z].astype(F32)
    for i in range(7):
        total = total + z_recv[i].astype(F32)
    part[...] = total

    here = 2 * core + y_lo
    whole[here] = total
    gathers = []
    for i in range(3):
        c = copy(part, whole.at[here], gather_send_sem.at[i], gather_recv_sem.at[i], group[i])
        c.start()
        gathers.append(c)

    wait_back(1)
    for lev in range(2):
        for left in (True, False):
            assemble(1, lev, left)

    for w in range(7):
        for k in range(2):
            forth(w, k, (a, up_b)).wait_send()
            back(w, k, (a, up_b)).wait_send()
    for j in range(3):
        forth7(j).wait_send()
        for k in range(2):
            back7(j, k).wait_send()
    for c in pairs + [relay_up, relay_dn, ring_up_b, ring_dn_a, ring_up_a, ring_dn_b] + lines + columns:
        c.wait_send()
    for c in gathers:
        c.wait_recv()
    for owner in range(2):
        at = owner * 768
        gq_ref[:, at : at + 256] = whole[2 * owner, 0:8, :]
        gq_ref[:, at + 256 : at + 512] = whole[2 * owner, 8:16, :]
        gq_ref[:, at + 512 : at + 768] = whole[2 * owner + 1, 0:8, :]
        go_ref[:, owner * 256 : owner * 256 + 256] = whole[2 * owner + 1, 8:16, :]
    for c in gathers:
        c.wait_send()
    for c in stores:
        c.wait()


def move_kernel(*refs):
    sources, targets, held, in_sem, out_sem = refs[:4], refs[4:8], refs[8:12], refs[12], refs[13]
    moves = []
    for i in range(4):
        for part in range(2) if i < 2 else (0,):
            n = len(moves)
            views = [ref.at[part] if i < 2 else ref for ref in (sources[i], held[i], targets[i])]
            first = pltpu.make_async_copy(views[0], views[1], in_sem.at[n])
            second = pltpu.make_async_copy(views[1], views[2], out_sem.at[n])
            first.start()
            moves.append((first, second))
    for first, second in moves:
        first.wait()
        second.start()
    for first, second in moves:
        second.wait()


def body(inputs, cotangent, w_qkv, w_out, gain, logit_scale):
    vmem = pl.BlockSpec(memory_space=pltpu.VMEM)
    smem = pl.BlockSpec(memory_space=pltpu.SMEM)
    dma = pltpu.SemaphoreType.DMA
    anywhere = pl.BlockSpec(memory_space=pl.ANY)
    halves = pltpu.VMEM((8, 2, 80, WIDTH), BF)
    pieces = pltpu.VMEM((3, 80, WIDTH), BF)
    quarters = pltpu.VMEM((3, 2, 48, WIDTH), BF)
    x_view = inputs.transpose(0, 2, 1, 3)
    g_view = cotangent.transpose(0, 2, 1, 3)
    out, grad_in, share_qkv, share_out = pl.pallas_call(
        block_kernel,
        out_shape=[
            jax.ShapeDtypeStruct(x_view.shape, BF),
            jax.ShapeDtypeStruct(x_view.shape, BF),
            jax.ShapeDtypeStruct((8, 3 * WIDTH), F32),
            jax.ShapeDtypeStruct((8, WIDTH), F32),
        ],
        in_specs=[anywhere] * 4 + [vmem, smem],
        out_specs=[anywhere] * 2 + [vmem] * 2,
        scratch_shapes=[
            pltpu.VMEM(x_view.shape, BF),
            pltpu.VMEM(x_view.shape, BF),
            pltpu.VMEM(w_qkv.shape, BF),
            pltpu.VMEM(w_out.shape, BF),
            pltpu.VMEM(x_view.shape, BF),
            pltpu.VMEM(x_view.shape, BF),
        ]
        + [halves] * 6
        + [pieces] * 2
        + [quarters] * 2
        + [
            pltpu.VMEM((8 * TOK, WIDTH), BF),
            pltpu.VMEM((8 * TOK, WIDTH), BF),
            pltpu.VMEM((8 * TOK, WIDTH), BF),
            pltpu.VMEM((8 * TOK, 3 * WIDTH), BF),
            pltpu.VMEM((3 * WIDTH, WIDTH), BF),
            pltpu.VMEM((WIDTH, WIDTH), BF),
            pltpu.VMEM((KEYS, 256), BF),
            pltpu.VMEM((256, KEYS), BF),
            pltpu.VMEM((256, 256), BF),
            pltpu.VMEM((2, KEYS), F32),
            pltpu.VMEM((2, 256), F32),
            pltpu.VMEM((2, 4, 4, 8, 16, 256), BF),
            pltpu.VMEM((4, 4, 8, 16, 256), BF),
            pltpu.VMEM((4, 4, 8, 16, 256), BF),
            pltpu.VMEM((2, 2, 8, 16, 256), BF),
            pltpu.VMEM((2, 4, 8, 16, 256), BF),
            pltpu.VMEM((4, 8, 16, 256), BF),
            pltpu.VMEM((3, 8, 16, 256), BF),
            pltpu.VMEM((8, 16, 256), BF),
            pltpu.VMEM((7, 16, 256), BF),
            pltpu.VMEM((16, 256), F32),
            pltpu.VMEM((4, 16, 256), F32),
        ]
        + [dma((7, 2))] * 4
        + [dma((3,))] * 2
        + [dma((3, 2))] * 2
        + [dma((4,))] * 2
        + [dma((2,))] * 2
        + [dma((4,))] * 2
        + [dma((3,))] * 2
        + [dma((7,))] * 2
        + [dma((3,))] * 2
        + [dma((4,)), dma((8,))],
        compiler_params=pltpu.CompilerParams(
            collective_id=0, has_side_effects=True, vmem_limit_bytes=56 * 2**20
        ),
    )(x_view, g_view, w_qkv, w_out, gain.reshape(1, WIDTH), logit_scale)
    results = (out, grad_in, share_qkv, share_out)
    out, grad_in, share_qkv, share_out = pl.pallas_call(
        move_kernel,
        out_shape=[jax.ShapeDtypeStruct(r.shape, r.dtype) for r in results],
        in_specs=[anywhere] * 4,
        out_specs=[anywhere] * 4,
        scratch_shapes=[pltpu.VMEM(r.shape, r.dtype) for r in results] + [dma((6,)), dma((6,))],
    )(*results)
    return out.transpose(0, 2, 1, 3), grad_in.transpose(0, 2, 1, 3), share_qkv, share_out.T


def solution(mesh):
    placed = (P(None, "lat", "lon", None), P(None, "lat", "lon", None), P(), P(), P(), P())
    return jax.shard_map(
        body,
        mesh=mesh,
        in_specs=placed,
        out_specs=(
            P(None, "lat", "lon", None),
            P(None, "lat", "lon", None),
            P("lon", None),
            P(None, "lon"),
        ),
        check_vma=False,
    )
```
